32 devices in a mesh: tp: 4 (over y, core), ep: 8 (over z, x).
Axes of the slice: x: 2, y: 2, z: 4, core: 2. Of those that a mesh axis runs over, the one named last changes fastest.
Arguments:
- tokens: bfloat16 [128, 8192], P('ep'), may hold values from -6 to 6
- cotangent: bfloat16 [128, 8192], P('ep'), may hold values from -6 to 6
- w_gate: bfloat16 [1792, 8192], P(('tp', 'ep')), may hold values from -0.0625 to 0.0625
- w_up: bfloat16 [1792, 8192], P(('tp', 'ep')), may hold values from -0.0625 to 0.0625
- w_down: bfloat16 [1792, 8192], P(('tp', 'ep')), may hold values from -0.5 to 0.5
- neuron_expert: int32 [1792], P(('tp', 'ep')), may hold values from 0 to 15, as said below
- neuron_slot: int32 [1792], P(('tp', 'ep')), may hold values from 0 to 55, as said below
- choice_expert: int32 [128, 8], P('ep'), may hold values from 0 to 15, all different within a row; in each aligned block of 16 rows (0 to 15, 16 to 31, ...) at most 16 rows name the same one
- choice_weight: float32 [128, 8], P('ep'), may hold values from 0.02 to 0.3
Outputs:
- output: bfloat16 [128, 8192], P('ep', 'tp')
- d_tokens: bfloat16 [128, 8192], P('ep', 'tp')
- d_weight: float32 [128, 8], P('ep')
- d_gate_exp: bfloat16 [16, 224, 8192], P('ep', 'tp')
- d_up_exp: bfloat16 [16, 224, 8192], P('ep', 'tp')
- d_down_exp: bfloat16 [16, 224, 8192], P('ep', 'tp')
The draws below stay inside these ranges and needn't reach their ends.
Inputs may be any that keep to these rules, and one draw needn't show every extreme that they name: `neuron_expert`: expert e belongs to ep index e // 2. Among the 56 neurons starting at any multiple of 56, at most 14 name experts of one ep index. `neuron_slot`: within each tp range of 448 neurons, the neurons of one expert have distinct slots. `choice_expert`: each row names 8 different experts; in each aligned block of 16 rows no expert is named more than 16 times.
All inputs are finite; a program needn't handle non-finite values.
Results may differ from the reference program's by a relative error of at most 0.018.
Values may be sent and summed in bfloat16 or wider, within the bound.
A program may use at most 128 MiB of HBM per device.

```python
import math
import jax
import jax.numpy as jnp
import numpy as np
from jax import lax

D = 8192
NL = 56
E_DEV = 2
TOPK = 8
TOK_DEV = 16
FF = 1792
EXPERTS = 16
PEER = 14
CAPN = 56
HID = 224
TCAP = 16
TOKENS = 128
N_TP = 4
N_EP = 8


def neuron_tables(key):
    base = jax.random.fold_in(key, 7)

    def one_group(group_key):
        key_hot, key_source, key_flip = jax.random.split(group_key, 3)
        hot = jax.random.randint(key_hot, (), 0, N_EP)
        others = (hot + 1 + jnp.repeat(jnp.arange(N_EP - 1, dtype=jnp.int32), PEER)) % N_EP

        def one_source(source_key):
            key_pick, key_order = jax.random.split(source_key)
            picked = jax.random.permutation(key_pick, others)[:NL - PEER]
            owners = jnp.concatenate([jnp.full((PEER,), hot, jnp.int32), picked.astype(jnp.int32)])
            return jax.random.permutation(key_order, owners)
        owners = jax.vmap(one_source)(jax.random.split(key_source, N_EP)).reshape(-1)
        onehot = (owners[:, None] == jnp.arange(N_EP, dtype=jnp.int32)[None, :]).astype(jnp.int32)
        before = jnp.cumsum(onehot, 0) - onehot
        rank = jnp.sum(before * onehot, 1)
        flip = jax.random.randint(key_flip, (N_EP,), 0, E_DEV)
        local = (rank + flip[owners]) % E_DEV
        return (owners * E_DEV + local, rank // E_DEV)
    experts, slots = jax.vmap(one_group)(jax.random.split(base, N_TP))
    return (experts.reshape(-1).astype(jnp.int32), slots.reshape(-1).astype(jnp.int32))


def draw_neuron_expert(key, part):
    return neuron_tables(key)[0]


def draw_neuron_slot(key, part):
    return neuron_tables(key)[1]


def levels(stream_key, shape, shards, low, largest):
    gain, own = 1.0, jax.random.fold_in(stream_key, 6)
    for dim, blocks in shards:
        heights = jnp.exp(jax.random.uniform(jax.random.fold_in(own, dim), (blocks,), jnp.float32, low / len(shards), largest / len(shards)))
        gain = gain * jnp.repeat(heights, shape[dim] // blocks).reshape([-1 if axis == dim else 1 for axis in range(len(shape))])
    return gain


def deal_out(rng, own, number, rows, amount, top, most, slope):
    sequence = jax.random.permutation(rng, amount)
    packed, ordinary = load_shares(amount, rows * top, most, slope, True), load_shares(amount, rows * top, most, slope, False)
    places = jnp.arange(amount)

    def named(lengths, turn):
        used = int((lengths > 0).sum())
        fixed = max(1, used // 4)
        passed = fixed + (places - fixed + turn * (used - fixed)) % max(1, amount - fixed)
        return jnp.zeros((amount,), jnp.int32).at[sequence[jnp.where(places < fixed, places, passed)]].set(jnp.asarray(lengths, jnp.int32))

    lengths = jnp.where(number % 4 == 0, named(packed, number // 4), named(ordinary, number - number // 4 - 1))
    mixed = jax.random.permutation(jax.random.fold_in(own, 3), amount)
    source_of, receiver = mixed[0:amount // 2 * 2:2], mixed[1:amount // 2 * 2:2]
    room = jnp.minimum(lengths[source_of] - 1, most - lengths[receiver]) // 2
    room = jnp.where((source_of == sequence[0]) | (receiver == sequence[0]) | (lengths[receiver] == 0), 0, jnp.maximum(room, 0))
    passed = jax.random.randint(jax.random.fold_in(own, 4), (amount // 2,), 0, 1 << 20) % (room + 1)
    lengths = lengths.at[source_of].add(-passed).at[receiver].add(passed)
    members = jnp.searchsorted(jnp.cumsum(lengths), jnp.arange(rows * top), side="right").astype(jnp.int32)
    grid = members.reshape(top, rows).T
    grid = grid[jax.random.permutation(jax.random.fold_in(own, 1), rows)]
    turn = jax.random.randint(jax.random.fold_in(own, 2), (rows, 1), 0, top)
    return jnp.take_along_axis(grid, (jnp.arange(top)[None, :] + turn) % top, axis=1)


def load_shares(count, total, limit, slope, full):
    weights = [(1 << 20) // math.isqrt(standing ** slope) + 1 for standing in range(1, count + 1)]
    largest = limit if full else min(limit, max(-(-total // count), total * weights[0] // sum(weights)))
    least = 1 if total - largest >= count - 1 else 0
    given, rest = [largest] + [least] * (count - 1), total - largest - least * (count - 1)
    while rest > 0:
        movable = [i for i in range(1, count) if given[i] < largest] or [i for i in range(1, count) if given[i] < limit]
        mass, budget = sum([weights[i] for i in movable]), rest
        for i in movable:
            more = min(limit - given[i], max(1, budget * weights[i] // mass), rest)
            given[i] = given[i] + more
            rest = rest - more
    return np.array(given)


def normal_values(rng, dims, width, bound, cuts=(), held_as=jnp.bfloat16):
    level = levels(rng, dims, cuts, -0.22, 0.18) if cuts else 1.0
    entries = jax.random.normal(rng, dims, jnp.float32) * width * level
    return jnp.minimum(jnp.maximum(entries, -bound), bound).astype(held_as)


def setup_inputs(seed: int = 0) -> dict:
    seeds = jax.random.split(jax.random.key(seed), 10)
    tokens = normal_values(seeds[0], (TOKENS, D), 1.0, 6.0, ((0, 8),))
    cotangent = normal_values(seeds[1], (TOKENS, D), 1.0, 6.0, ((0, 8),))
    w_gate = normal_values(seeds[2], (FF, D), D ** -0.5, 0.0625, ((0, 32),))
    w_up = normal_values(seeds[3], (FF, D), D ** -0.5, 0.0625, ((0, 32),))
    w_down = normal_values(seeds[4], (FF, D), (NL * N_TP // E_DEV) ** -0.5, 0.5, ((0, 32),))
    neuron_expert = draw_neuron_expert(jax.random.fold_in(seeds[9], 71), 0)
    neuron_slot = draw_neuron_slot(jax.random.fold_in(seeds[9], 71), 0)
    choice_expert_keys = jax.random.split(jax.random.fold_in(seeds[7], 1), TOKENS // TOK_DEV)
    choice_expert_turns = jax.random.permutation(jax.random.fold_in(seeds[7], 3), TOKENS // TOK_DEV)
    choice_expert = jax.vmap(lambda own, number: deal_out(jax.random.fold_in(seeds[7], 2), own, number, TOK_DEV, EXPERTS, TOPK, TCAP, 1))(choice_expert_keys, choice_expert_turns).reshape((TOKENS, TOPK))
    choice_weight = jnp.clip(0.02 + 0.28 * jax.random.uniform(seeds[8], (TOKENS, TOPK), jnp.float32) ** levels(seeds[8], (TOKENS, TOPK), ((0, 8),), -0.2, 0.2), 0.02, 0.3)
    return {"tokens": tokens, "cotangent": cotangent, "w_gate": w_gate, "w_up": w_up, "w_down": w_down, "neuron_expert": neuron_expert, "neuron_slot": neuron_slot, "choice_expert": choice_expert, "choice_weight": choice_weight}


def slope_of(gate):
    sig = jax.nn.sigmoid(gate)
    return sig * (1.0 + gate * (1.0 - sig))


def block_sums(pairs):
    total = None
    for left, right in pairs:
        parts = jnp.einsum('rtc,tcd->rtd', left.reshape(-1, N_TP, CAPN).astype(jnp.float32), right.reshape(N_TP, CAPN, D).astype(jnp.float32))
        total = parts if total is None else total + parts
    rounded = lax.optimization_barrier(total.astype(jnp.bfloat16))
    return jnp.sum(rounded.astype(jnp.float32), 1)


def reference(tokens, cotangent, w_gate, w_up, w_down, neuron_expert, neuron_slot, choice_expert, choice_weight):
    neuron = jnp.arange(FF, dtype=jnp.int32)
    dest = (neuron_expert * HID + (neuron // (FF // N_TP)) * CAPN + neuron_slot).astype(jnp.int32)

    def layout(weight):
        return jnp.zeros((EXPERTS * HID, D), jnp.bfloat16).at[dest].set(weight).reshape(EXPERTS, HID, D)

    gate_exp = layout(w_gate)
    up_exp = layout(w_up)
    down_exp = layout(w_down)
    count = TOK_DEV * TOPK
    flat = choice_expert.reshape(N_EP, count)
    row_iota = lax.broadcasted_iota(jnp.int32, (count, count), 0)
    col_iota = lax.broadcasted_iota(jnp.int32, (count, count), 1)
    same = (flat[:, :, None] == flat[:, None, :]) & (col_iota < row_iota)[None]
    rank = jnp.sum(same.astype(jnp.int32), 2)
    source = jnp.arange(N_EP, dtype=jnp.int32)[:, None]
    slot_index = ((flat * N_EP + source) * TCAP + rank).reshape(-1).astype(jnp.int32)
    token_index = (jnp.arange(TOKENS * TOPK, dtype=jnp.int32) // TOPK).astype(jnp.int32)
    rows_expert = N_EP * TCAP
    x_disp = jnp.zeros((EXPERTS * rows_expert, D), jnp.bfloat16).at[slot_index].set(tokens[token_index]).reshape(EXPERTS, rows_expert, D)

    def forward(items):
        x_rows, w_g, w_u, w_d = items
        gate = jnp.dot(x_rows, w_g.T, preferred_element_type=jnp.float32)
        upper = jnp.dot(x_rows, w_u.T, preferred_element_type=jnp.float32)
        hidden = (jax.nn.silu(gate) * upper).astype(jnp.bfloat16)
        result = block_sums([(hidden, w_d)]).astype(jnp.bfloat16)
        return result, gate, upper

    outs, gates, uppers = lax.map(forward, (x_disp, gate_exp, up_exp, down_exp))
    per_choice = outs.reshape(-1, D)[slot_index].astype(jnp.float32).reshape(TOKENS, TOPK, D)
    output = jnp.sum(choice_weight[:, :, None] * per_choice, 1).astype(jnp.bfloat16)
    d_weight = jnp.sum(per_choice * cotangent.astype(jnp.float32)[:, None, :], 2)
    scaled = (choice_weight[:, :, None] * cotangent.astype(jnp.float32)[:, None, :]).astype(jnp.bfloat16).reshape(-1, D)
    g_disp = jnp.zeros((EXPERTS * rows_expert, D), jnp.bfloat16).at[slot_index].set(scaled).reshape(EXPERTS, rows_expert, D)

    def backward(items):
        x_rows, g_rows, gate, upper, w_g, w_u, w_d = items
        hidden = (jax.nn.silu(gate) * upper).astype(jnp.bfloat16)
        d_hidden = jnp.dot(g_rows, w_d.T, preferred_element_type=jnp.float32)
        d_down = jnp.dot(hidden.T, g_rows, preferred_element_type=jnp.float32).astype(jnp.bfloat16)
        d_gate_rows = (d_hidden * upper * slope_of(gate)).astype(jnp.bfloat16)
        d_up_rows = (d_hidden * jax.nn.silu(gate)).astype(jnp.bfloat16)
        d_gate = jnp.dot(d_gate_rows.T, x_rows, preferred_element_type=jnp.float32).astype(jnp.bfloat16)
        d_up = jnp.dot(d_up_rows.T, x_rows, preferred_element_type=jnp.float32).astype(jnp.bfloat16)
        d_rows = block_sums([(d_gate_rows, w_g), (d_up_rows, w_u)]).astype(jnp.bfloat16)
        return d_rows, d_gate, d_up, d_down

    d_rows, d_gate_exp, d_up_exp, d_down_exp = lax.map(backward, (x_disp, g_disp, gates, uppers, gate_exp, up_exp, down_exp))
    d_choice = d_rows.reshape(-1, D)[slot_index].astype(jnp.float32).reshape(TOKENS, TOPK, D)
    d_tokens = jnp.sum(d_choice, 1).astype(jnp.bfloat16)
    return output, d_tokens, d_weight, d_gate_exp, d_up_exp, d_down_exp
```

```python
import jax
import jax.numpy as jnp
from jax import lax
from jax.sharding import PartitionSpec as P

E_DEV = 2


def body(tokens, cotangent, w_gate, w_up, w_down, neuron_expert, neuron_slot, choice_expert, choice_weight):
    n_ep = lax.axis_size("ep")
    experts = E_DEV * n_ep
    neurons = w_gate.shape[0]
    peer_slots = 2 * ((neurons + n_ep - 1) // n_ep)
    capacity = n_ep * peer_slots // E_DEV
    bf16, f32 = jnp.bfloat16, jnp.float32

    expert_ids = jnp.arange(experts, dtype=jnp.int32)
    named = choice_expert[:, :, None] == expert_ids[None, None, :]
    weight_local = jnp.sum(jnp.where(named, choice_weight[:, :, None], 0.0), 1)
    weight_all = lax.all_gather(weight_local, "ep", axis=0, tiled=True)
    x_all = lax.all_gather(tokens, "ep", axis=0, tiled=True)
    c_all = lax.all_gather(cotangent, "ep", axis=0, tiled=True)
    labels = neuron_expert * capacity + neuron_slot
    labels_all = lax.all_gather(labels, "ep", axis=0, tiled=True)

    def rows_by_tokens(rows, wide):
        return jnp.einsum("nd,td->nt", rows, wide, preferred_element_type=f32)

    gate = rows_by_tokens(w_gate, x_all)
    upper = rows_by_tokens(w_up, x_all)
    value = rows_by_tokens(w_down, c_all)
    weight = jnp.take(weight_all, neuron_expert, axis=1).T
    sig = jax.nn.sigmoid(gate)
    silu = gate * sig
    hidden = silu * upper
    d_hidden = weight * value
    scaled = (weight * hidden).astype(bf16)
    d_gate = (d_hidden * upper * (sig * (1.0 + gate * (1.0 - sig)))).astype(bf16)
    d_up = (d_hidden * silu).astype(bf16)

    factors = jnp.concatenate([scaled, d_gate, d_up], 1)
    factors_all = lax.all_gather(factors, "ep", axis=0, tiled=True)

    def from_neurons(factor, rows):
        return jnp.einsum("nt,nd->td", factor, rows, preferred_element_type=f32)

    output = from_neurons(scaled, w_down).astype(bf16)
    d_tokens = (from_neurons(d_gate, w_gate) + from_neurons(d_up, w_up)).astype(bf16)

    def to_owner(rows):
        part = lax.psum_scatter(rows, "tp", scatter_dimension=1, tiled=True)
        return lax.psum_scatter(part, "ep", scatter_dimension=0, tiled=True)

    output = to_owner(output)
    d_tokens = to_owner(d_tokens)

    member = (neuron_expert[:, None] == expert_ids[None, :]).astype(f32)
    per_expert = jnp.einsum(
        "nt,ne->te", hidden * value, member, preferred_element_type=f32, precision=lax.Precision.HIGHEST
    )
    per_expert = lax.psum(per_expert, ("tp", "ep"))
    mine = lax.dynamic_slice_in_dim(per_expert, lax.axis_index("ep") * tokens.shape[0], tokens.shape[0], 0)
    d_weight = jnp.sum(jnp.where(named, mine[:, None, :], 0.0), 2)

    slots = E_DEV * capacity
    slot_of = labels_all - lax.axis_index("ep") * slots
    placing = (jnp.arange(slots, dtype=jnp.int32)[:, None] == slot_of[None, :]).astype(bf16)
    placed = jnp.dot(placing, factors_all, preferred_element_type=f32).astype(bf16)
    count = x_all.shape[0]

    def gradient(index, wide):
        factor = placed[:, index * count : (index + 1) * count]
        grad = jnp.dot(factor, wide, preferred_element_type=f32).astype(bf16)
        return grad.reshape(E_DEV, capacity, -1)

    return output, d_tokens, d_weight, gradient(1, x_all), gradient(2, x_all), gradient(0, c_all)


def solution(mesh):
    in_specs = (
        P("ep", None),
        P("ep", None),
        P(("tp", "ep"), None),
        P(("tp", "ep"), None),
        P(("tp", "ep"), None),
        P(("tp", "ep")),
        P(("tp", "ep")),
        P("ep", None),
        P("ep", None),
    )
    out_specs = (
        P("ep", "tp"),
        P("ep", "tp"),
        P("ep", None),
        P("ep", "tp", None),
        P("ep", "tp", None),
        P("ep", "tp", None),
    )
    return jax.shard_map(body, mesh=mesh, in_specs=in_specs, out_specs=out_specs, check_vma=False)
```

```python
import functools

import jax
import jax.numpy as jnp
from jax import lax
from jax.experimental import pallas as pl
from jax.experimental.pallas import tpu as pltpu
from jax.sharding import PartitionSpec as P

E_DEV = 2
CORES = 2
LANES = 128
PACK = 16
MESH = pl.DeviceIdType.MESH
BF16, F32 = jnp.bfloat16, jnp.float32


def grid_of(n_tp, n_ep):
    n_x = 1
    while 8 * n_x * n_x <= n_ep:
        n_x *= 2
    return n_tp // CORES, n_ep // n_x, n_x


def each(low, high, step):
    def run(i, carry):
        step(i)
        return carry

    if high - low == 1:
        step(low)
    elif high > low:
        lax.fori_loop(low, high, run, 0)


def dot(left, right, dims, precision=None):
    return lax.dot_general(left, right, (dims, ((), ())), precision=precision, preferred_element_type=F32)


def kernel(
    n_tp, n_ep, tok, cot, wg, wu, wd, we, member, pack, label,
    out, dtok, dwt, grad_gate, grad_up, grad_down,
    xs, cs, wa, fs, fr, sw, rw, rv, part, rc, ry, rx, rz, grads,
    s_z, s_x, s_y, s_c, r_ag, s_w, r_w, s_f, r_f, s_s, r_s, s_v, r_v,
    s_rc, r_rc, s_ry, r_ry, s_rx, r_rx, s_rz, r_rz, s_g,
):
    n_y, n_z, n_x = grid_of(n_tp, n_ep)
    t, p = lax.axis_index("tp"), lax.axis_index("ep")
    y, c = t // CORES, lax.rem(t, CORES)
    z, x = p // n_x, lax.rem(p, n_x)
    other = 1 - c
    rows, width = tok.shape
    count = n_ep * rows
    quarter = width // n_tp
    group = n_z * rows
    bufs = (xs, cs)

    def place(z_, x_):
        return x_ * n_z + z_

    def at(z_, x_):
        return (t, z_ * n_x + x_)

    def ep_peer(i):
        return lax.rem(p + 1 + i, n_ep)

    def place_of(p_):
        return place(p_ // n_x, lax.rem(p_, n_x))

    def copy(src, dst, send, recv, device):
        return pltpu.make_async_remote_copy(
            src_ref=src, dst_ref=dst, send_sem=send, recv_sem=recv, device_id=device, device_id_type=MESH
        )

    def got(dst, recv, device):
        copy(dst, dst, s_v.at[0], recv, device).wait_recv()

    here = place(z, x)

    def rows_at(i, size):
        return pl.ds(pl.multiple_of(i * size, size), size)

    def cols_at(q):
        return pl.ds(pl.multiple_of(q * quarter, LANES), quarter)

    def block(a, k, q):
        return bufs[a].at[rows_at(k, rows), cols_at(q)]

    def ranked(k):
        return place(lax.rem(z + n_z - lax.rem(k, n_z), n_z), lax.rem(x + k // n_z, n_x))

    def z_send(a, i):
        b = block(a, here, t)
        return copy(b, b, s_z.at[a, i], r_ag.at[a, here, t], at(lax.rem(z + 1 + i, n_z), x))

    def x_send(a, k, i):
        b = block(a, ranked(k), t)
        return copy(b, b, s_x.at[a, k, i], r_ag.at[a, ranked(k), t], at(z, lax.rem(x + 1 + i, n_x)))

    def y_send(a, k, i):
        b = block(a, ranked(k), t)
        to = lax.rem(y + 1 + i, n_y) * CORES + c
        return copy(b, b, s_y.at[a, k, i], r_ag.at[a, ranked(k), t], (to, p))

    def c_send(a, k, qy):
        q = qy * CORES + c
        b = block(a, ranked(k), q)
        return copy(b, b, s_c.at[a, k, qy], r_ag.at[a, ranked(k), q], (y * CORES + other, p))

    def arrived(a, k, q):
        got(block(a, ranked(k), q), r_ag.at[a, ranked(k), q], (y * CORES + other, p))

    def w_send(i):
        b = wa.at[rows_at(here, rows)]
        return copy(b, b, s_w.at[i], r_w.at[here], (t, ep_peer(i)))

    def f_send(i):
        to = ep_peer(i)
        return copy(fs.at[rows_at(to, PACK)], fr.at[rows_at(p, PACK)], s_f.at[i], r_f.at[p], (t, to))

    def s_send(i):
        to = ep_peer(i)
        return copy(sw.at[rows_at(place_of(to), rows)], rw.at[p], s_s.at[i], r_s.at[p], (t, to))

    def v_send(i):
        to = lax.rem(t + 1 + i, n_tp)
        return copy(rv.at[t], rv.at[t], s_v.at[i], r_v.at[t], (to, p))

    def rc_send(a, qy, g):
        src = part.at[a, qy * CORES + other, rows_at(g, group)]
        return copy(src, rc.at[a, qy, g], s_rc.at[a, qy, g], r_rc.at[a, qy, g], (y * CORES + other, p))

    def ry_send(a, i, g):
        to = lax.rem(y + 1 + i, n_y) * CORES + c
        src = part.at[a, to, rows_at(g, group)]
        return copy(src, ry.at[a, n_y - 2 - i, g], s_ry.at[a, i, g], r_ry.at[a, n_y - 2 - i, g], (to, p))

    def rx_send(a, i):
        to = lax.rem(x + 1 + i, n_x)
        src = part.at[a, t, rows_at(to, group)]
        return copy(src, rx.at[a, x], s_rx.at[a, i], r_rx.at[a, x], at(z, to))

    def rz_send(a, i):
        to = lax.rem(z + 1 + i, n_z)
        src = part.at[a, t, rows_at(place(to, x), rows)]
        return copy(src, rz.at[a, z], s_rz.at[a, i], r_rz.at[a, z], at(to, x))

    barrier = pltpu.get_barrier_semaphore()
    each(0, n_ep - 1, lambda i: pl.semaphore_signal(barrier, inc=1, device_id=(t, ep_peer(i)), device_id_type=MESH))
    each(
        0, n_tp - 1,
        lambda i: pl.semaphore_signal(barrier, inc=1, device_id=(lax.rem(t + 1 + i, n_tp), p), device_id_type=MESH),
    )
    xs[rows_at(here, rows)] = tok[...]
    cs[rows_at(here, rows)] = cot[...]
    wa[rows_at(here, rows)] = we[...]
    pl.semaphore_wait(barrier, n_ep - 1 + n_tp - 1)

    for a in range(2):
        each(0, n_z - 1, lambda i: z_send(a, i).start())
        each(0, n_x - 1, lambda i: x_send(a, 0, i).start())
    each(0, n_ep - 1, lambda i: w_send(i).start())

    def forward(a):
        def near(k):
            arrived(a, k, t)
            each(0, n_x - 1, lambda i: x_send(a, k, i).start())
            each(0, n_y - 1, lambda i: y_send(a, k, i).start())
            c_send(a, k, y).start()

        def far(k):
            arrived(a, k, t)
            each(0, n_y - 1, lambda i: y_send(a, k, i).start())
            c_send(a, k, y).start()

        each(1, n_z, near)
        each(n_z, n_ep, far)

    def across(a):
        def from_y(i):
            qy = lax.rem(y + 1 + i, n_y)

            def one(k):
                arrived(a, k, qy * CORES + c)
                c_send(a, k, qy).start()

            each(1, n_ep, one)

        each(0, n_y - 1, from_y)

    def finish(a):
        each(0, n_y, lambda qy: each(1, n_ep, lambda k: arrived(a, k, qy * CORES + other)))

    def rows_by_tokens(weight, wide):
        def step(q, total):
            return total + dot(weight[:, cols_at(q)], wide[:, cols_at(q)], ((1,), (1,)))

        return lax.fori_loop(0, n_tp, step, jnp.zeros((weight.shape[0], count), F32))

    step_cols = min(quarter, 512)

    def spread(a, pairs):
        def one(q):
            def chunk(j):
                at_cols = pl.ds(pl.multiple_of(q * quarter + j * step_cols, LANES), step_cols)
                total = None
                for factor, weight in pairs:
                    term = dot(factor, weight[:, at_cols], ((1,), (0,)))
                    total = term if total is None else total + term
                part[a, q, :, pl.ds(pl.multiple_of(j * step_cols, LANES), step_cols)] = total.astype(BF16)

            each(0, quarter // step_cols, chunk)

        def away(i):
            qy = lax.rem(y + 1 + i, n_y)
            one(qy * CORES + other)
            each(0, n_x, lambda g: rc_send(a, qy, lax.rem(x + 1 + g, n_x)).start())

        each(0, n_y, away)
        each(0, n_y, lambda i: one(lax.rem(y + 1 + i, n_y) * CORES + c))

    def add_into(a, q, base, ref):
        def some(j):
            span = rows_at(base + j, rows)
            part[a, q, span] = (
                part[a, q, span].astype(F32) + ref[rows_at(j, rows)].astype(F32)
            ).astype(BF16)

        each(0, ref.shape[0] // rows, some)

    def reduce_core(a):
        def one(gi):
            g = lax.rem(x + 1 + gi, n_x)

            def turn(i):
                qy = lax.rem(y + 1 + i, n_y)
                got(rc.at[a, qy, g], r_rc.at[a, qy, g], (y * CORES + other, p))
                add_into(a, qy * CORES + c, g * n_z, rc.at[a, qy, g])

            def send(i):
                turn(i)
                ry_send(a, i, g).start()

            each(0, n_y - 1, send)
            turn(n_y - 1)

        each(0, n_x, one)

    def reduce_y(a):
        def one(g):
            def add(i):
                qy = lax.rem(y + 1 + i, n_y)
                got(ry.at[a, i, g], r_ry.at[a, i, g], (qy * CORES + c, p))
                add_into(a, t, g * n_z, ry.at[a, i, g])

            each(0, n_y - 1, add)

        def send(i):
            one(lax.rem(x + 1 + i, n_x))
            rx_send(a, i).start()

        each(0, n_x - 1, send)
        one(x)

    def reduce_x(a):
        def add(i):
            from_x = lax.rem(x + 1 + i, n_x)
            got(rx.at[a, from_x], r_rx.at[a, from_x], at(z, from_x))
            add_into(a, t, x * n_z, rx.at[a, from_x])

        each(0, n_x - 1, add)
        each(0, n_z - 1, lambda i: rz_send(a, i).start())

    def reduce_z(a, result):
        total = part[a, t, rows_at(here, rows)].astype(F32)
        for i in range(n_z - 1):
            from_z = lax.rem(z + 1 + i, n_z)
            got(rz.at[a, from_z], r_rz.at[a, from_z], at(from_z, x))
            total = total + rz[a, from_z].astype(F32)
        result[...] = total.astype(BF16)

    exact = lax.Precision.HIGHEST
    forward(0)
    forward(1)
    across(0)
    finish(0)
    gate = rows_by_tokens(wg, xs)
    upper = rows_by_tokens(wu, xs)
    each(0, n_ep - 1, lambda i: got(wa.at[rows_at(place_of(ep_peer(i)), rows)], r_w.at[place_of(ep_peer(i))], (t, ep_peer(i))))
    weight = dot(member[...], wa[...], ((1,), (1,)), exact)
    sig = 1.0 / (1.0 + jnp.exp(-gate))
    silu = gate * sig
    hidden = silu * upper
    scaled = weight * hidden
    spread(0, [(scaled.T.astype(BF16), wd)])
    across(1)
    reduce_core(0)
    finish(1)
    value = rows_by_tokens(wd, cs)
    d_hidden = weight * value
    d_gate = d_hidden * upper * (sig * (1.0 + gate * (1.0 - sig)))
    d_up = d_hidden * silu
    factors = jnp.concatenate([scaled.astype(BF16), d_gate.astype(BF16), d_up.astype(BF16), label[...]], 1)
    fs[...] = dot(pack[...], factors, ((1,), (0,))).astype(BF16)
    each(0, n_ep - 1, lambda i: f_send(i).start())
    spread(1, [(d_gate.T.astype(BF16), wg), (d_up.T.astype(BF16), wu)])
    reduce_y(0)
    sw[...] = dot((hidden * value).T, member[...], ((1,), (0,)), exact)
    each(0, n_ep - 1, lambda i: s_send(i).start())
    rw[p] = sw[rows_at(here, rows)]
    reduce_core(1)
    reduce_x(0)
    fr[rows_at(p, PACK)] = fs[rows_at(p, PACK)]
    each(0, n_ep - 1, lambda i: got(fr.at[rows_at(ep_peer(i), PACK)], r_f.at[ep_peer(i)], (t, ep_peer(i))))
    slots = grads.shape[1]
    slot_ids = lax.broadcasted_iota(jnp.int32, (n_ep * PACK, LANES), 1).astype(F32) + 1.0
    chosen = jnp.where(fr[:, 3 * count :].astype(F32) == slot_ids, 1.0, 0.0)
    placing = chosen.T.astype(BF16)[:slots]
    placed = dot(placing, fr[:, : 3 * count], ((1,), (0,))).astype(BF16)

    keep = grads.shape[0]
    stores = []
    for index, wide, ref in ((1, xs, grad_gate), (2, xs, grad_up), (0, cs, grad_down)):
        slot = len(stores) % keep
        if len(stores) >= keep:
            stores[len(stores) - keep].wait()
        factor = placed[:, index * count : (index + 1) * count]

        def gradient(j):
            span = pl.ds(pl.multiple_of(j * step_cols, LANES), step_cols)
            grads[slot, :, span] = dot(factor, wide[:, span], ((1,), (0,))).astype(BF16)

        each(0, width // step_cols, gradient)
        stores.append(pltpu.make_async_copy(grads.at[slot], ref, s_g.at[len(stores)]))
        stores[-1].start()
    reduce_y(1)
    each(0, n_ep - 1, lambda i: got(rw.at[ep_peer(i)], r_s.at[ep_peer(i)], (t, ep_peer(i))))
    rv[t] = jnp.sum(rw[...], 0)
    each(0, n_tp - 1, lambda i: v_send(i).start())
    reduce_x(1)
    reduce_z(0, out)

    def v_got(i):
        source = lax.rem(t + 1 + i, n_tp)
        got(rv.at[source], r_v.at[source], (source, p))

    each(0, n_tp - 1, v_got)
    dwt[...] = jnp.sum(rv[...], 0)
    reduce_z(1, dtok)
    for store in stores[-keep:]:
        store.wait()
    each(0, n_ep - 1, lambda i: w_send(i).wait_send())
    each(0, n_ep - 1, lambda i: f_send(i).wait_send())
    each(0, n_ep - 1, lambda i: s_send(i).wait_send())
    each(0, n_tp - 1, lambda i: v_send(i).wait_send())
    for a in range(2):
        each(0, n_z - 1, lambda i: z_send(a, i).wait_send())
        each(0, n_z, lambda k: each(0, n_x - 1, lambda i: x_send(a, k, i).wait_send()))
        each(1, n_ep, lambda k: each(0, n_y - 1, lambda i: y_send(a, k, i).wait_send()))
        each(1, n_ep, lambda k: each(0, n_y, lambda q: c_send(a, k, q).wait_send()))
        each(0, n_y, lambda q: each(0, n_x, lambda g: rc_send(a, q, g).wait_send()))
        each(0, n_y - 1, lambda i: each(0, n_x, lambda g: ry_send(a, i, g).wait_send()))
        each(0, n_x - 1, lambda i: rx_send(a, i).wait_send())
        each(0, n_z - 1, lambda i: rz_send(a, i).wait_send())


def earlier_same(labels):
    count = labels.shape[0]
    row_iota = lax.broadcasted_iota(jnp.int32, (count, count), 0)
    col_iota = lax.broadcasted_iota(jnp.int32, (count, count), 1)
    same = (labels[:, None] == labels[None, :]) & (col_iota < row_iota)
    return jnp.sum(same.astype(jnp.int32), 1)


def body(tokens, cotangent, w_gate, w_up, w_down, neuron_expert, neuron_slot, choice_expert, choice_weight):
    n_ep, n_tp = lax.axis_size("ep"), lax.axis_size("tp")
    n_y, n_z, n_x = grid_of(n_tp, n_ep)
    neurons, width = w_gate.shape
    rows = tokens.shape[0]
    count = n_ep * rows
    quarter = width // n_tp
    group = n_z * rows
    peer_slots = 2 * ((neurons + n_ep - 1) // n_ep)
    capacity = n_ep * peer_slots // E_DEV
    slots = E_DEV * capacity
    assert peer_slots <= PACK and slots <= LANES and E_DEV * n_ep <= LANES

    ids = jnp.arange(LANES, dtype=jnp.int32)
    named = choice_expert[:, :, None] == ids[None, None, :]
    by_expert = jnp.sum(jnp.where(named, choice_weight[:, :, None], 0.0), 1)
    member = (neuron_expert[:, None] == ids[None, :]).astype(F32)
    owner = neuron_expert // E_DEV
    target = owner * PACK + earlier_same(owner)
    pack = (jnp.arange(n_ep * PACK, dtype=jnp.int32)[:, None] == target[None, :]).astype(BF16)
    label = (neuron_expert % E_DEV * capacity + neuron_slot + 1).astype(F32).astype(BF16)
    label = jnp.broadcast_to(label[:, None], (neurons, LANES))

    keep = 3 if count <= 2 * LANES else 2
    vmem = pl.BlockSpec(memory_space=pltpu.VMEM)
    anywhere = pl.BlockSpec(memory_space=pl.ANY)
    dma = pltpu.SemaphoreType.DMA
    small = jax.ShapeDtypeStruct((rows, quarter), BF16)
    grad = jax.ShapeDtypeStruct((slots, width), BF16)
    output, d_tokens, per_expert, d_gate, d_up, d_down = pl.pallas_call(
        functools.partial(kernel, n_tp, n_ep),
        out_shape=(small, small, jax.ShapeDtypeStruct((rows, LANES), F32), grad, grad, grad),
        in_specs=[vmem] * 9,
        out_specs=[vmem] * 3 + [anywhere] * 3,
        scratch_shapes=[
            pltpu.VMEM((count, width), BF16),
            pltpu.VMEM((count, width), BF16),
            pltpu.VMEM((count, LANES), F32),
            pltpu.VMEM((n_ep * PACK, 3 * count + LANES), BF16),
            pltpu.VMEM((n_ep * PACK, 3 * count + LANES), BF16),
            pltpu.VMEM((count, LANES), F32),
            pltpu.VMEM((n_ep, rows, LANES), F32),
            pltpu.VMEM((n_tp, rows, LANES), F32),
            pltpu.VMEM((2, n_tp, count, quarter), BF16),
            pltpu.VMEM((2, n_y, n_x, group, quarter), BF16),
            pltpu.VMEM((2, n_y - 1, n_x, group, quarter), BF16),
            pltpu.VMEM((2, n_x, group, quarter), BF16),
            pltpu.VMEM((2, n_z, rows, quarter), BF16),
            pltpu.VMEM((keep, slots, width), BF16),
            dma((2, n_z)),
            dma((2, n_z, n_x)),
            dma((2, n_ep, n_y)),
            dma((2, n_ep, n_y)),
            dma((2, n_ep, n_tp)),
            dma((n_ep,)),
            dma((n_ep,)),
            dma((n_ep,)),
            dma((n_ep,)),
            dma((n_ep,)),
            dma((n_ep,)),
            dma((n_tp,)),
            dma((n_tp,)),
            dma((2, n_y, n_x)),
            dma((2, n_y, n_x)),
            dma((2, n_y, n_x)),
            dma((2, n_y, n_x)),
            dma((2, n_x)),
            dma((2, n_x)),
            dma((2, n_z)),
            dma((2, n_z)),
            dma((3,)),
        ],
        compiler_params=pltpu.CompilerParams(
            collective_id=0, has_side_effects=True, vmem_limit_bytes=62 * 1024 * 1024
        ),
    )(tokens, cotangent, w_gate, w_up, w_down, by_expert, member, pack, label)
    d_weight = jnp.sum(jnp.where(named, per_expert[:, None, :], 0.0), 2)

    def expert_blocks(rows_):
        return rows_.reshape(E_DEV, capacity, width)

    return output, d_tokens, d_weight, expert_blocks(d_gate), expert_blocks(d_up), expert_blocks(d_down)


def solution(mesh):
    in_specs = (
        P("ep", None),
        P("ep", None),
        P(("tp", "ep"), None),
        P(("tp", "ep"), None),
        P(("tp", "ep"), None),
        P(("tp", "ep")),
        P(("tp", "ep")),
        P("ep", None),
        P("ep", None),
    )
    out_specs = (
        P("ep", "tp"),
        P("ep", "tp"),
        P("ep", None),
        P("ep", "tp", None),
        P("ep", "tp", None),
        P("ep", "tp", None),
    )
    return jax.shard_map(body, mesh=mesh, in_specs=in_specs, out_specs=out_specs, check_vma=False)
```

```python
import functools

import jax
import jax.numpy as jnp
from jax import lax
from jax.experimental import pallas as pl
from jax.experimental.pallas import tpu as pltpu
from jax.sharding import PartitionSpec as P

E_DEV = 2
CORES = 2
LANES = 128
PACK = 16
MESH = pl.DeviceIdType.MESH
BF16, F32 = jnp.bfloat16, jnp.float32


def grid_of(n_tp, n_ep):
    n_x = 1
    while 8 * n_x * n_x <= n_ep:
        n_x *= 2
    return n_tp // CORES, n_ep // n_x, n_x


def each(low, high, step):
    def run(i, carry):
        step(i)
        return carry

    if high - low == 1:
        step(low)
    elif high > low:
        lax.fori_loop(low, high, run, 0)


def dot(left, right, dims, precision=None):
    return lax.dot_general(left, right, (dims, ((), ())), precision=precision, preferred_element_type=F32)


def kernel(
    n_tp, n_ep, tok, cot, wg, wu, wd, ne, ns, ce, cw,
    out, dtok, dwt, grad_gate, grad_up, grad_down,
    xs, cs, wa, fs, fr, sw, rw, rv, part, rc, ry, rx, rz, grads,
    s_z, s_zs, s_x, s_xs, s_y, s_c, s_cs, r_ag, r_sd, s_w, r_w, s_f, r_f, s_s, r_s, s_v, r_v,
    s_rc, r_rc, s_ry, r_ry, s_rx, r_rx, s_rz, r_rz, s_g,
):
    n_y, n_z, n_x = grid_of(n_tp, n_ep)
    t, p = lax.axis_index("tp"), lax.axis_index("ep")
    y, c = t // CORES, lax.rem(t, CORES)
    z, x = p // n_x, lax.rem(p, n_x)
    other = 1 - c
    rows, width = tok.shape
    count = n_ep * rows
    quarter = width // n_tp
    group = n_z * rows
    bufs = (xs, cs)

    def place(z_, x_):
        return x_ * n_z + z_

    def at(z_, x_):
        return (t, z_ * n_x + x_)

    def ep_peer(i):
        return lax.rem(p + 1 + i, n_ep)

    def place_of(p_):
        return place(p_ // n_x, lax.rem(p_, n_x))

    def copy(src, dst, send, recv, device):
        return pltpu.make_async_remote_copy(
            src_ref=src, dst_ref=dst, send_sem=send, recv_sem=recv, device_id=device, device_id_type=MESH
        )

    def got(dst, recv, device):
        copy(dst, dst, s_v.at[0], recv, device).wait_recv()

    here = place(z, x)

    def rows_at(i, size):
        return pl.ds(pl.multiple_of(i * size, size), size)

    def cols_at(q):
        return pl.ds(pl.multiple_of(q * quarter, LANES), quarter)

    side = quarter // 2

    def block(a, k, q):
        return bufs[a].at[rows_at(k, rows), cols_at(q)]

    def side_block(a, k, q):
        return bufs[a].at[rows_at(k, rows), pl.ds(pl.multiple_of(q * quarter, LANES), side)]

    def rest_block(a, k, q):
        return bufs[a].at[rows_at(k, rows), pl.ds(pl.multiple_of(q * quarter + side, LANES), quarter - side)]

    def ranked(k):
        return place(lax.rem(z + n_z - lax.rem(k, n_z), n_z), lax.rem(x + k // n_z, n_x))

    def next_y(i):
        return lax.rem(y + 1 + i, n_y)

    sibling = (y * CORES + other, p)

    def z_send(a, i):
        b = block(a, here, t)
        return copy(b, b, s_z.at[a, i], r_ag.at[a, here, t], at(lax.rem(z + 1 + i, n_z), x))

    def zs_send(a, i, j):
        q = next_y(j) * CORES + c
        b = side_block(a, here, q)
        return copy(b, b, s_zs.at[a, i, j], r_sd.at[a, here, q], at(lax.rem(z + 1 + i, n_z), x))

    def x_send(a, k, i):
        b = block(a, ranked(k), t)
        return copy(b, b, s_x.at[a, k, i], r_ag.at[a, ranked(k), t], at(z, lax.rem(x + 1 + i, n_x)))

    def xs_send(a, k, i, j):
        q = next_y(j) * CORES + c
        b = side_block(a, ranked(k), q)
        return copy(b, b, s_xs.at[a, k, i, j], r_sd.at[a, ranked(k), q], at(z, lax.rem(x + 1 + i, n_x)))

    def y_send(a, k, i):
        b = rest_block(a, ranked(k), t)
        return copy(b, b, s_y.at[a, k, i], r_ag.at[a, ranked(k), t], (next_y(i) * CORES + c, p))

    def c_send(a, k):
        b = block(a, ranked(k), t)
        return copy(b, b, s_c.at[a, k, n_y - 1], r_ag.at[a, ranked(k), t], sibling)

    def cr_send(a, k, i):
        q = next_y(i) * CORES + c
        b = rest_block(a, ranked(k), q)
        return copy(b, b, s_c.at[a, k, i], r_ag.at[a, ranked(k), q], sibling)

    def cs_send(a, k, i):
        q = next_y(i) * CORES + c
        b = side_block(a, ranked(k), q)
        return copy(b, b, s_cs.at[a, k, i], r_sd.at[a, ranked(k), q], sibling)

    def arrived(a, k, q):
        got(block(a, ranked(k), q), r_ag.at[a, ranked(k), q], sibling)

    def side_arrived(a, k, q):
        got(side_block(a, ranked(k), q), r_sd.at[a, ranked(k), q], sibling)

    def rest_arrived(a, k, q):
        got(rest_block(a, ranked(k), q), r_ag.at[a, ranked(k), q], sibling)

    def w_send(i):
        b = wa.at[rows_at(here, rows)]
        return copy(b, b, s_w.at[i], r_w.at[here], (t, ep_peer(i)))

    def f_send(i):
        to = ep_peer(i)
        return copy(fs.at[rows_at(to, PACK)], fr.at[rows_at(p, PACK)], s_f.at[i], r_f.at[p], (t, to))

    def s_send(i):
        to = ep_peer(i)
        return copy(sw.at[rows_at(place_of(to), rows)], rw.at[p], s_s.at[i], r_s.at[p], (t, to))

    def v_send(i):
        to = lax.rem(t + 1 + i, n_tp)
        return copy(rv.at[t], rv.at[t], s_v.at[i], r_v.at[t], (to, p))

    def rc_send(a, qy, g):
        src = part.at[a, qy * CORES + other, rows_at(g, group)]
        return copy(src, rc.at[a, qy, g], s_rc.at[a, qy, g], r_rc.at[a, qy, g], (y * CORES + other, p))

    def ry_send(a, i, g):
        to = lax.rem(y + 1 + i, n_y) * CORES + c
        src = part.at[a, to, rows_at(g, group)]
        return copy(src, ry.at[a, n_y - 2 - i, g], s_ry.at[a, i, g], r_ry.at[a, n_y - 2 - i, g], (to, p))

    def rx_send(a, i):
        to = lax.rem(x + 1 + i, n_x)
        src = part.at[a, t, rows_at(to, group)]
        return copy(src, rx.at[a, x], s_rx.at[a, i], r_rx.at[a, x], at(z, to))

    def rz_send(a, i):
        to = lax.rem(z + 1 + i, n_z)
        src = part.at[a, t, rows_at(place(to, x), rows)]
        return copy(src, rz.at[a, z], s_rz.at[a, i], r_rz.at[a, z], at(to, x))

    barrier = pltpu.get_barrier_semaphore()
    each(0, n_ep - 1, lambda i: pl.semaphore_signal(barrier, inc=1, device_id=(t, ep_peer(i)), device_id_type=MESH))
    each(
        0, n_tp - 1,
        lambda i: pl.semaphore_signal(barrier, inc=1, device_id=(lax.rem(t + 1 + i, n_tp), p), device_id_type=MESH),
    )
    xs[rows_at(here, rows)] = tok[...]
    cs[rows_at(here, rows)] = cot[...]
    pl.semaphore_wait(barrier, n_ep - 1 + n_tp - 1)

    for a in range(2):
        each(0, n_z - 1, lambda i: z_send(a, i).start())
        each(0, n_x - 1, lambda i: x_send(a, 0, i).start())
        each(0, n_z - 1, lambda i: each(0, n_y - 1, lambda j: zs_send(a, i, j).start()))
        each(0, n_x - 1, lambda i: each(0, n_y - 1, lambda j: xs_send(a, 0, i, j).start()))

    experts = lax.broadcasted_iota(jnp.int32, (rows, LANES), 1)
    by_expert = jnp.zeros((rows, LANES), F32)
    for k in range(ce.shape[1]):
        by_expert = by_expert + jnp.where(ce[:, k : k + 1] == experts, cw[:, k : k + 1], 0.0)
    wa[rows_at(here, rows)] = by_expert
    each(0, n_ep - 1, lambda i: w_send(i).start())

    neurons = wg.shape[0]
    slots = grads.shape[1]
    named = ne[...]
    owner = lax.div(named, E_DEV)

    def ids(size):
        return lax.broadcasted_iota(jnp.int32, (size, neurons), 0)

    def ones(mask):
        return jnp.where(mask, 1.0, 0.0)

    member = ones(ids(LANES) == named).T
    owned = ones(ids(n_ep) == owner)
    order = ones(ids(neurons) < lax.broadcasted_iota(jnp.int32, (neurons, neurons), 1))
    before = dot(owned.astype(BF16), order.astype(BF16), ((1,), (0,)))
    target = owner.astype(F32) * PACK + jnp.sum(owned * before, 0, keepdims=True)
    pack = ones(ids(n_ep * PACK).astype(F32) == target).astype(BF16)
    label = (lax.rem(named, E_DEV) * (slots // E_DEV) + ns[...] + 1).astype(F32)
    label = jnp.broadcast_to(label, (LANES, neurons)).T.astype(BF16)

    def forward(a, k, near):
        arrived(a, k, t)
        if near:
            each(0, n_x - 1, lambda i: x_send(a, k, i).start())
        each(0, n_y - 1, lambda i: y_send(a, k, i).start())
        c_send(a, k).start()

        def one(j):
            side_arrived(a, k, next_y(j) * CORES + c)
            if near:
                each(0, n_x - 1, lambda i: xs_send(a, k, i, j).start())
            cs_send(a, k, j).start()

        each(0, n_y - 1, one)

    def across(a, k):
        def one(i):
            rest_arrived(a, k, next_y(i) * CORES + c)
            cr_send(a, k, i).start()

        each(0, n_y - 1, one)

    def project(a, weights):
        def add(q, totals):
            wide = bufs[a][:, cols_at(q)]
            return tuple(total + dot(weight[:, cols_at(q)], wide, ((1,), (1,))) for total, weight in zip(totals, weights))

        def mine(i, totals):
            return add(lax.rem(y + i, n_y) * CORES + c, totals)

        def theirs(i, totals):
            q = next_y(i) * CORES + other

            def one(k):
                rest_arrived(a, k, q)
                side_arrived(a, k, q)

            each(1, n_ep, one)
            return add(q, totals)

        totals = tuple(jnp.zeros((neurons, count), F32) for _ in weights)
        totals = lax.fori_loop(0, n_y, mine, totals)
        each(1, n_ep, lambda k: arrived(a, k, y * CORES + other))
        totals = add(y * CORES + other, totals)
        return lax.fori_loop(0, n_y - 1, theirs, totals)

    step_cols = min(quarter, 512)

    def spread(a, pairs):
        def one(q):
            def chunk(j):
                at_cols = pl.ds(pl.multiple_of(q * quarter + j * step_cols, LANES), step_cols)
                total = None
                for factor, weight in pairs:
                    term = dot(factor, weight[:, at_cols], ((1,), (0,)))
                    total = term if total is None else total + term
                part[a, q, :, pl.ds(pl.multiple_of(j * step_cols, LANES), step_cols)] = total.astype(BF16)

            each(0, quarter // step_cols, chunk)

        def away(i):
            qy = lax.rem(y + 1 + i, n_y)
            one(qy * CORES + other)
            each(0, n_x, lambda g: rc_send(a, qy, lax.rem(x + 1 + g, n_x)).start())

        each(0, n_y, away)
        each(0, n_y, lambda i: one(lax.rem(y + 1 + i, n_y) * CORES + c))

    def add_into(a, q, base, ref):
        def some(j):
            span = rows_at(base + j, rows)
            part[a, q, span] = (
                part[a, q, span].astype(F32) + ref[rows_at(j, rows)].astype(F32)
            ).astype(BF16)

        each(0, ref.shape[0] // rows, some)

    def reduce_core(a):
        def one(gi):
            g = lax.rem(x + 1 + gi, n_x)

            def turn(i):
                qy = lax.rem(y + 1 + i, n_y)
                got(rc.at[a, qy, g], r_rc.at[a, qy, g], (y * CORES + other, p))
                add_into(a, qy * CORES + c, g * n_z, rc.at[a, qy, g])

            def send(i):
                turn(i)
                ry_send(a, i, g).start()

            each(0, n_y - 1, send)
            turn(n_y - 1)

        each(0, n_x, one)

    def reduce_y(a):
        def one(g):
            def add(i):
                qy = lax.rem(y + 1 + i, n_y)
                got(ry.at[a, i, g], r_ry.at[a, i, g], (qy * CORES + c, p))
                add_into(a, t, g * n_z, ry.at[a, i, g])

            each(0, n_y - 1, add)

        def send(i):
            one(lax.rem(x + 1 + i, n_x))
            rx_send(a, i).start()

        each(0, n_x - 1, send)
        one(x)

    def reduce_x(a):
        def add(i):
            from_x = lax.rem(x + 1 + i, n_x)
            got(rx.at[a, from_x], r_rx.at[a, from_x], at(z, from_x))
            add_into(a, t, x * n_z, rx.at[a, from_x])

        each(0, n_x - 1, add)
        each(0, n_z - 1, lambda i: rz_send(a, i).start())

    def reduce_z(a, result):
        total = part[a, t, rows_at(here, rows)].astype(F32)
        for i in range(n_z - 1):
            from_z = lax.rem(z + 1 + i, n_z)
            got(rz.at[a, from_z], r_rz.at[a, from_z], at(from_z, x))
            total = total + rz[a, from_z].astype(F32)
        result[...] = total.astype(BF16)

    exact = lax.Precision.HIGHEST
    each(1, n_z, lambda k: forward(0, k, True))
    each(n_z, n_ep, lambda k: forward(0, k, False))

    def both(k, near):
        across(0, k)
        forward(1, k, near)

    each(1, n_z, lambda k: both(k, True))
    each(n_z, n_ep, lambda k: both(k, False))
    gate, upper = project(0, (wg, wu))
    each(0, n_ep - 1, lambda i: got(wa.at[rows_at(place_of(ep_peer(i)), rows)], r_w.at[place_of(ep_peer(i))], (t, ep_peer(i))))
    weight = dot(member, wa[...], ((1,), (1,)), exact)
    sig = 1.0 / (1.0 + jnp.exp(-gate))
    silu = gate * sig
    hidden = silu * upper
    scaled = weight * hidden
    spread(0, [(scaled.T.astype(BF16), wd)])
    each(1, n_ep, lambda k: across(1, k))
    reduce_core(0)
    (value,) = project(1, (wd,))
    d_hidden = weight * value
    d_gate = d_hidden * upper * (sig * (1.0 + gate * (1.0 - sig)))
    d_up = d_hidden * silu
    factors = jnp.concatenate([scaled.astype(BF16), d_gate.astype(BF16), d_up.astype(BF16), label], 1)
    fs[...] = dot(pack, factors, ((1,), (0,))).astype(BF16)
    each(0, n_ep - 1, lambda i: f_send(i).start())
    spread(1, [(d_gate.T.astype(BF16), wg), (d_up.T.astype(BF16), wu)])
    reduce_y(0)
    sw[...] = dot((hidden * value).T, member, ((1,), (0,)), exact)
    each(0, n_ep - 1, lambda i: s_send(i).start())
    rw[p] = sw[rows_at(here, rows)]
    reduce_core(1)
    reduce_x(0)
    fr[rows_at(p, PACK)] = fs[rows_at(p, PACK)]
    each(0, n_ep - 1, lambda i: got(fr.at[rows_at(ep_peer(i), PACK)], r_f.at[ep_peer(i)], (t, ep_peer(i))))
    slot_ids = lax.broadcasted_iota(jnp.int32, (n_ep * PACK, LANES), 1).astype(F32) + 1.0
    chosen = jnp.where(fr[:, 3 * count :].astype(F32) == slot_ids, 1.0, 0.0)
    placing = chosen.T.astype(BF16)[:slots]
    placed = dot(placing, fr[:, : 3 * count], ((1,), (0,))).astype(BF16)

    keep = grads.shape[0]
    stores = []
    for index, wide, ref in ((1, xs, grad_gate), (2, xs, grad_up), (0, cs, grad_down)):
        slot = len(stores) % keep
        if len(stores) >= keep:
            stores[len(stores) - keep].wait()
        factor = placed[:, index * count : (index + 1) * count]

        def gradient(j):
            span = pl.ds(pl.multiple_of(j * step_cols, LANES), step_cols)
            grads[slot, :, span] = dot(factor, wide[:, span], ((1,), (0,))).astype(BF16)

        each(0, width // step_cols, gradient)
        stores.append(pltpu.make_async_copy(grads.at[slot], ref, s_g.at[len(stores)]))
        stores[-1].start()
    reduce_y(1)
    each(0, n_ep - 1, lambda i: got(rw.at[ep_peer(i)], r_s.at[ep_peer(i)], (t, ep_peer(i))))
    rv[t] = jnp.sum(rw[...], 0)
    each(0, n_tp - 1, lambda i: v_send(i).start())
    reduce_x(1)
    reduce_z(0, out)

    def v_got(i):
        source = lax.rem(t + 1 + i, n_tp)
        got(rv.at[source], r_v.at[source], (source, p))

    each(0, n_tp - 1, v_got)
    per_expert = jnp.sum(rv[...], 0)
    choice = lax.broadcasted_iota(jnp.int32, dwt.shape, 1)
    picked = jnp.zeros(dwt.shape, F32)
    for k in range(ce.shape[1]):
        value_k = jnp.sum(jnp.where(ce[:, k : k + 1] == experts, per_expert, 0.0), 1, keepdims=True)
        picked = picked + jnp.where(choice == k, value_k, 0.0)
    dwt[...] = picked
    reduce_z(1, dtok)
    for store in stores[-keep:]:
        store.wait()
    each(0, n_ep - 1, lambda i: w_send(i).wait_send())
    each(0, n_ep - 1, lambda i: f_send(i).wait_send())
    each(0, n_ep - 1, lambda i: s_send(i).wait_send())
    each(0, n_tp - 1, lambda i: v_send(i).wait_send())
    for a in range(2):
        each(0, n_z - 1, lambda i: z_send(a, i).wait_send())
        each(0, n_z - 1, lambda i: each(0, n_y - 1, lambda j: zs_send(a, i, j).wait_send()))

        def row_sent(k):
            def one(i):
                x_send(a, k, i).wait_send()
                each(0, n_y - 1, lambda j: xs_send(a, k, i, j).wait_send())

            each(0, n_x - 1, one)

        def block_sent(k):
            def one(i):
                y_send(a, k, i).wait_send()
                cr_send(a, k, i).wait_send()
                cs_send(a, k, i).wait_send()

            c_send(a, k).wait_send()
            each(0, n_y - 1, one)

        each(0, n_z, row_sent)
        each(1, n_ep, block_sent)
        each(0, n_y, lambda q: each(0, n_x, lambda g: rc_send(a, q, g).wait_send()))
        each(0, n_y - 1, lambda i: each(0, n_x, lambda g: ry_send(a, i, g).wait_send()))
        each(0, n_x - 1, lambda i: rx_send(a, i).wait_send())
        each(0, n_z - 1, lambda i: rz_send(a, i).wait_send())


def hand_on(*refs):
    arrays, sems = refs[:-1], refs[-1]
    half = len(arrays) // 2
    small, large = slice(0, 3), slice(3, half)
    stores = [
        pltpu.make_async_copy(src, dst, sems.at[i])
        for i, (src, dst) in enumerate(zip(arrays[:half][large], arrays[half:][large]))
    ]
    for store in stores:
        store.start()
    for src, dst in zip(arrays[:half][small], arrays[half:][small]):
        dst[...] = src[...]
    for store in stores:
        store.wait()


def body(tokens, cotangent, w_gate, w_up, w_down, neuron_expert, neuron_slot, choice_expert, choice_weight):
    n_ep, n_tp = lax.axis_size("ep"), lax.axis_size("tp")
    n_y, n_z, n_x = grid_of(n_tp, n_ep)
    neurons, width = w_gate.shape
    rows = tokens.shape[0]
    count = n_ep * rows
    quarter = width // n_tp
    group = n_z * rows
    peer_slots = 2 * ((neurons + n_ep - 1) // n_ep)
    capacity = n_ep * peer_slots // E_DEV
    slots = E_DEV * capacity
    assert peer_slots <= PACK and slots <= LANES and E_DEV * n_ep <= LANES

    keep = 3 if count <= 2 * LANES else 2
    vmem = pl.BlockSpec(memory_space=pltpu.VMEM)
    anywhere = pl.BlockSpec(memory_space=pl.ANY)
    dma = pltpu.SemaphoreType.DMA
    small = jax.ShapeDtypeStruct((rows, quarter), BF16)
    grad = jax.ShapeDtypeStruct((slots, width), BF16)
    shapes = (small, small, jax.ShapeDtypeStruct(choice_weight.shape, F32), grad, grad, grad)
    results = pl.pallas_call(
        functools.partial(kernel, n_tp, n_ep),
        out_shape=shapes,
        in_specs=[vmem] * 9,
        out_specs=[vmem] * 3 + [anywhere] * 3,
        scratch_shapes=[
            pltpu.VMEM((count, width), BF16),
            pltpu.VMEM((count, width), BF16),
            pltpu.VMEM((count, LANES), F32),
            pltpu.VMEM((n_ep * PACK, 3 * count + LANES), BF16),
            pltpu.VMEM((n_ep * PACK, 3 * count + LANES), BF16),
            pltpu.VMEM((count, LANES), F32),
            pltpu.VMEM((n_ep, rows, LANES), F32),
            pltpu.VMEM((n_tp, rows, LANES), F32),
            pltpu.VMEM((2, n_tp, count, quarter), BF16),
            pltpu.VMEM((2, n_y, n_x, group, quarter), BF16),
            pltpu.VMEM((2, n_y - 1, n_x, group, quarter), BF16),
            pltpu.VMEM((2, n_x, group, quarter), BF16),
            pltpu.VMEM((2, n_z, rows, quarter), BF16),
            pltpu.VMEM((keep, slots, width), BF16),
            dma((2, n_z)),
            dma((2, n_z, n_y)),
            dma((2, n_z, n_x)),
            dma((2, n_z, n_x, n_y)),
            dma((2, n_ep, n_y)),
            dma((2, n_ep, n_y)),
            dma((2, n_ep, n_y)),
            dma((2, n_ep, n_tp)),
            dma((2, n_ep, n_tp)),
            dma((n_ep,)),
            dma((n_ep,)),
            dma((n_ep,)),
            dma((n_ep,)),
            dma((n_ep,)),
            dma((n_ep,)),
            dma((n_tp,)),
            dma((n_tp,)),
            dma((2, n_y, n_x)),
            dma((2, n_y, n_x)),
            dma((2, n_y, n_x)),
            dma((2, n_y, n_x)),
            dma((2, n_x)),
            dma((2, n_x)),
            dma((2, n_z)),
            dma((2, n_z)),
            dma((3,)),
        ],
        compiler_params=pltpu.CompilerParams(
            collective_id=0, has_side_effects=True, vmem_limit_bytes=62 * 1024 * 1024
        ),
    )(
        tokens, cotangent, w_gate, w_up, w_down,
        neuron_expert.reshape(1, -1), neuron_slot.reshape(1, -1), choice_expert, choice_weight,
    )
    output, d_tokens, d_weight, d_gate, d_up, d_down = pl.pallas_call(
        hand_on,
        out_shape=shapes,
        in_specs=[vmem] * 3 + [anywhere] * 3,
        out_specs=[vmem] * 3 + [anywhere] * 3,
        scratch_shapes=[dma((3,))],
    )(*results)

    def expert_blocks(rows_):
        return rows_.reshape(E_DEV, capacity, width)

    return output, d_tokens, d_weight, expert_blocks(d_gate), expert_blocks(d_up), expert_blocks(d_down)


def solution(mesh):
    in_specs = (
        P("ep", None),
        P("ep", None),
        P(("tp", "ep"), None),
        P(("tp", "ep"), None),
        P(("tp", "ep"), None),
        P(("tp", "ep")),
        P(("tp", "ep")),
        P("ep", None),
        P("ep", None),
    )
    out_specs = (
        P("ep", "tp"),
        P("ep", "tp"),
        P("ep", None),
        P("ep", "tp", None),
        P("ep", "tp", None),
        P("ep", "tp", None),
    )
    return jax.shard_map(body, mesh=mesh, in_specs=in_specs, out_specs=out_specs, check_vma=False)
```

```python
import functools

import jax
import jax.numpy as jnp
from jax import lax
from jax.experimental import pallas as pl
from jax.experimental.pallas import tpu as pltpu
from jax.sharding import PartitionSpec as P

E_DEV = 2
CORES = 2
LANES = 128
PACK = 16
MESH = pl.DeviceIdType.MESH
BF16, F32 = jnp.bfloat16, jnp.float32


def grid_of(n_tp, n_ep):
    n_x = 1
    while 8 * n_x * n_x <= n_ep:
        n_x *= 2
    return n_tp // CORES, n_ep // n_x, n_x


def each(low, high, step):
    def run(i, carry):
        step(i)
        return carry

    if high - low == 1:
        step(low)
    elif high > low:
        lax.fori_loop(low, high, run, 0)


def dot(left, right, dims, precision=None):
    return lax.dot_general(left, right, (dims, ((), ())), precision=precision, preferred_element_type=F32)


def kernel(
    n_tp, n_ep, tok, cot, wg, wu, wd, ne, ns, ce, cw,
    out, dtok, dwt, placed, x_out, c_out,
    xs, cs, wa, fs, fr, sw, rw, rv, part, rc, ry, rx, rz,
    s_z, s_x, s_y, s_c, r_ag, r_sd, r_c, s_w, r_w, s_f, r_f, s_s, r_s, s_v, r_v,
    s_rc, r_rc, s_ry, r_ry, s_rx, r_rx, s_rz, r_rz, s_g,
):
    n_y, n_z, n_x = grid_of(n_tp, n_ep)
    t, p = lax.axis_index("tp"), lax.axis_index("ep")
    y, c = t // CORES, lax.rem(t, CORES)
    z, x = p // n_x, lax.rem(p, n_x)
    other = 1 - c
    rows, width = tok.shape
    count = n_ep * rows
    quarter = width // n_tp
    group = n_z * rows
    bufs = (xs, cs)

    def place(z_, x_):
        return x_ * n_z + z_

    def at(z_, x_):
        return (t, z_ * n_x + x_)

    def ep_peer(i):
        return lax.rem(p + 1 + i, n_ep)

    def place_of(p_):
        return place(p_ // n_x, lax.rem(p_, n_x))

    def copy(src, dst, send, recv, device):
        return pltpu.make_async_remote_copy(
            src_ref=src, dst_ref=dst, send_sem=send, recv_sem=recv, device_id=device, device_id_type=MESH
        )

    def got(dst, recv, device):
        copy(dst, dst, s_v, recv, device).wait_recv()

    def taken(ref, sem):
        pltpu.make_async_copy(ref, ref, sem).wait()

    here = place(z, x)

    def rows_at(i, size):
        return pl.ds(pl.multiple_of(i * size, size), size)

    def cols_at(q):
        return pl.ds(pl.multiple_of(q * quarter, LANES), quarter)

    side = quarter // 2

    def block(a, k, q):
        return bufs[a].at[rows_at(k, rows), cols_at(q)]

    def side_block(a, k, q):
        return bufs[a].at[rows_at(k, rows), pl.ds(pl.multiple_of(q * quarter, LANES), side)]

    def rest_block(a, k, q):
        return bufs[a].at[rows_at(k, rows), pl.ds(pl.multiple_of(q * quarter + side, LANES), quarter - side)]

    def ranked(k):
        return place(lax.rem(z + n_z - lax.rem(k, n_z), n_z), lax.rem(x + k // n_z, n_x))

    def next_y(i):
        return lax.rem(y + 1 + i, n_y)

    sibling = (y * CORES + other, p)

    def z_send(a, i):
        b = block(a, here, t)
        return copy(b, b, s_z.at[a], r_ag.at[a, here, t], at(lax.rem(z + 1 + i, n_z), x))

    def zs_send(a, i, j):
        q = next_y(j) * CORES + c
        b = side_block(a, here, q)
        return copy(b, b, s_z.at[a], r_sd.at[a, here, q], at(lax.rem(z + 1 + i, n_z), x))

    def x_send(a, k, i):
        b = block(a, ranked(k), t)
        return copy(b, b, s_x.at[a], r_ag.at[a, ranked(k), t], at(z, lax.rem(x + 1 + i, n_x)))

    def xs_send(a, k, i, j):
        q = next_y(j) * CORES + c
        b = side_block(a, ranked(k), q)
        return copy(b, b, s_x.at[a], r_sd.at[a, ranked(k), q], at(z, lax.rem(x + 1 + i, n_x)))

    def y_send(a, k, i):
        b = rest_block(a, ranked(k), t)
        return copy(b, b, s_y.at[a], r_ag.at[a, ranked(k), t], (next_y(i) * CORES + c, p))

    def c_send(a, k, qy):
        b = block(a, ranked(k), qy * CORES + c)
        return copy(b, b, s_c.at[a], r_c.at[a], sibling)

    def arrived(a, k, q):
        got(block(a, ranked(k), q), r_ag.at[a, ranked(k), q], sibling)

    def side_arrived(a, k, q):
        got(side_block(a, ranked(k), q), r_sd.at[a, ranked(k), q], sibling)

    def rest_arrived(a, k, q):
        got(rest_block(a, ranked(k), q), r_ag.at[a, ranked(k), q], sibling)

    def w_send(i):
        b = wa.at[rows_at(here, rows)]
        return copy(b, b, s_w, r_w, (t, ep_peer(i)))

    def f_send(i):
        to = ep_peer(i)
        return copy(fs.at[rows_at(to, PACK)], fr.at[rows_at(p, PACK)], s_f, r_f, (t, to))

    def s_send(i):
        to = ep_peer(i)
        return copy(sw.at[rows_at(place_of(to), rows)], rw.at[p], s_s, r_s, (t, to))

    def v_send(i):
        to = lax.rem(t + 1 + i, n_tp)
        return copy(rv.at[t], rv.at[t], s_v, r_v, (to, p))

    def rc_send(a, qy, g):
        src = part.at[a, qy * CORES + other, rows_at(g, group)]
        return copy(src, rc.at[a, qy, g], s_rc.at[a], r_rc.at[a, qy, g], (y * CORES + other, p))

    def ry_send(a, i, g):
        to = lax.rem(y + 1 + i, n_y) * CORES + c
        src = part.at[a, to, rows_at(g, group)]
        return copy(src, ry.at[a, n_y - 2 - i, g], s_ry.at[a], r_ry.at[a, n_y - 2 - i, g], (to, p))

    def rx_send(a, i):
        to = lax.rem(x + 1 + i, n_x)
        src = part.at[a, t, rows_at(to, group)]
        return copy(src, rx.at[a, x], s_rx.at[a], r_rx.at[a, x], at(z, to))

    def rz_send(a, i):
        to = lax.rem(z + 1 + i, n_z)
        src = part.at[a, t, rows_at(place(to, x), rows)]
        return copy(src, rz.at[a, z], s_rz.at[a], r_rz.at[a, z], at(to, x))

    barrier = pltpu.get_barrier_semaphore()
    each(0, n_ep - 1, lambda i: pl.semaphore_signal(barrier, inc=1, device_id=(t, ep_peer(i)), device_id_type=MESH))
    each(
        0, n_tp - 1,
        lambda i: pl.semaphore_signal(barrier, inc=1, device_id=(lax.rem(t + 1 + i, n_tp), p), device_id_type=MESH),
    )
    xs[rows_at(here, rows)] = tok[...]
    cs[rows_at(here, rows)] = cot[...]
    pl.semaphore_wait(barrier, n_ep - 1 + n_tp - 1)

    for a in range(2):
        each(0, n_z - 1, lambda i: z_send(a, i).start())
        each(0, n_x - 1, lambda i: x_send(a, 0, i).start())
        each(0, n_z - 1, lambda i: each(0, n_y - 1, lambda j: zs_send(a, i, j).start()))
        each(0, n_x - 1, lambda i: each(0, n_y - 1, lambda j: xs_send(a, 0, i, j).start()))

    experts = lax.broadcasted_iota(jnp.int32, (rows, LANES), 1).astype(F32)
    by_expert = jnp.zeros((rows, LANES), F32)
    chosen_by, weight_by = ce[...].astype(F32).T, cw[...].T
    top = ce.shape[0]
    for k in range(top):
        by_expert = by_expert + jnp.where(chosen_by[:, k : k + 1] == experts, weight_by[:, k : k + 1], 0.0)
    wa[rows_at(here, rows)] = by_expert
    each(0, n_ep - 1, lambda i: w_send(i).start())

    neurons = wg.shape[0]
    slots = placed.shape[0]
    named = ne[...]
    owner = lax.div(named, E_DEV)

    def ids(size):
        return lax.broadcasted_iota(jnp.int32, (size, neurons), 0)

    def ones(mask):
        return jnp.where(mask, 1.0, 0.0)

    member = ones(ids(LANES) == named).T
    owned = ones(ids(n_ep) == owner)
    order = ones(ids(neurons) < lax.broadcasted_iota(jnp.int32, (neurons, neurons), 1))
    before = dot(owned.astype(BF16), order.astype(BF16), ((1,), (0,)))
    target = owner.astype(F32) * PACK + jnp.sum(owned * before, 0, keepdims=True)
    pack = ones(ids(n_ep * PACK).astype(F32) == target).astype(BF16)
    label = (lax.rem(named, E_DEV) * (slots // E_DEV) + ns[...] + 1).astype(F32)
    label = jnp.broadcast_to(label, (LANES, neurons)).T.astype(BF16)

    def forward(a, k, near):
        arrived(a, k, t)
        if near:
            each(0, n_x - 1, lambda i: x_send(a, k, i).start())
        each(0, n_y - 1, lambda i: y_send(a, k, i).start())
        c_send(a, k, y).start()

        def one(j):
            side_arrived(a, k, next_y(j) * CORES + c)
            if near:
                each(0, n_x - 1, lambda i: xs_send(a, k, i, j).start())

        each(0, n_y - 1, one)

    def across(a, k):
        def one(i):
            rest_arrived(a, k, next_y(i) * CORES + c)
            c_send(a, k, next_y(i)).start()

        each(0, n_y - 1, one)

    def project(a, weights):
        def add(q, totals):
            wide = bufs[a][:, cols_at(q)]
            return tuple(total + dot(weight[:, cols_at(q)], wide, ((1,), (1,))) for total, weight in zip(totals, weights))

        def mine(i, totals):
            return add(lax.rem(y + i, n_y) * CORES + c, totals)

        def theirs(i, totals):
            return add(lax.rem(y + i, n_y) * CORES + other, totals)

        totals = tuple(jnp.zeros((neurons, count), F32) for _ in weights)
        totals = lax.fori_loop(0, n_y, mine, totals)
        taken(bufs[a].at[pl.ds(0, count - rows), pl.ds(0, n_y * quarter)], r_c.at[a])
        return lax.fori_loop(0, n_y, theirs, totals)

    step_cols = min(quarter, 512)

    def spread(a, pairs):
        def one(q):
            def chunk(j):
                at_cols = pl.ds(pl.multiple_of(q * quarter + j * step_cols, LANES), step_cols)
                total = None
                for factor, weight in pairs:
                    term = dot(factor, weight[:, at_cols], ((1,), (0,)))
                    total = term if total is None else total + term
                part[a, q, :, pl.ds(pl.multiple_of(j * step_cols, LANES), step_cols)] = total.astype(BF16)

            each(0, quarter // step_cols, chunk)

        def away(i):
            qy = lax.rem(y + 1 + i, n_y)
            one(qy * CORES + other)
            each(0, n_x, lambda g: rc_send(a, qy, lax.rem(x + 1 + g, n_x)).start())

        each(0, n_y, away)
        each(0, n_y, lambda i: one(lax.rem(y + 1 + i, n_y) * CORES + c))

    def add_into(a, q, base, ref):
        def some(j):
            span = rows_at(base + j, rows)
            part[a, q, span] = (
                part[a, q, span].astype(F32) + ref[rows_at(j, rows)].astype(F32)
            ).astype(BF16)

        each(0, ref.shape[0] // rows, some)

    def reduce_core(a):
        def one(gi):
            g = lax.rem(x + 1 + gi, n_x)

            def turn(i):
                qy = lax.rem(y + 1 + i, n_y)
                got(rc.at[a, qy, g], r_rc.at[a, qy, g], (y * CORES + other, p))
                add_into(a, qy * CORES + c, g * n_z, rc.at[a, qy, g])

            def send(i):
                turn(i)
                ry_send(a, i, g).start()

            each(0, n_y - 1, send)
            turn(n_y - 1)

        each(0, n_x, one)

    def reduce_y(a):
        def one(g):
            def add(i):
                qy = lax.rem(y + 1 + i, n_y)
                got(ry.at[a, i, g], r_ry.at[a, i, g], (qy * CORES + c, p))
                add_into(a, t, g * n_z, ry.at[a, i, g])

            each(0, n_y - 1, add)

        def send(i):
            one(lax.rem(x + 1 + i, n_x))
            rx_send(a, i).start()

        each(0, n_x - 1, send)
        one(x)

    def reduce_x(a):
        def add(i):
            from_x = lax.rem(x + 1 + i, n_x)
            got(rx.at[a, from_x], r_rx.at[a, from_x], at(z, from_x))
            add_into(a, t, x * n_z, rx.at[a, from_x])

        each(0, n_x - 1, add)
        each(0, n_z - 1, lambda i: rz_send(a, i).start())

    def reduce_z(a, result):
        total = part[a, t, rows_at(here, rows)].astype(F32)
        for i in range(n_z - 1):
            from_z = lax.rem(z + 1 + i, n_z)
            got(rz.at[a, from_z], r_rz.at[a, from_z], at(from_z, x))
            total = total + rz[a, from_z].astype(F32)
        result[...] = total.astype(BF16)

    exact = lax.Precision.HIGHEST
    each(1, n_z, lambda k: forward(0, k, True))
    each(n_z, n_ep, lambda k: forward(0, k, False))

    def both(k, near):
        across(0, k)
        forward(1, k, near)

    each(1, n_z, lambda k: both(k, True))
    each(n_z, n_ep, lambda k: both(k, False))
    gate, upper = project(0, (wg, wu))
    stores = [pltpu.make_async_copy(buf, ref, s_g.at[i]) for i, (buf, ref) in enumerate(((xs, x_out), (cs, c_out)))]
    stores[0].start()
    taken(wa.at[pl.ds(0, count - rows)], r_w)
    weight = dot(member, wa[...], ((1,), (1,)), exact)
    sig = 1.0 / (1.0 + jnp.exp(-gate))
    silu = gate * sig
    hidden = silu * upper
    scaled = weight * hidden
    spread(0, [(scaled.T.astype(BF16), wd)])
    each(1, n_ep, lambda k: across(1, k))
    reduce_core(0)
    (value,) = project(1, (wd,))
    stores[1].start()
    d_hidden = weight * value
    d_gate = d_hidden * upper * (sig * (1.0 + gate * (1.0 - sig)))
    d_up = d_hidden * silu
    factors = jnp.concatenate([scaled.astype(BF16), d_gate.astype(BF16), d_up.astype(BF16), label], 1)
    fs[...] = dot(pack, factors, ((1,), (0,))).astype(BF16)
    each(0, n_ep - 1, lambda i: f_send(i).start())
    spread(1, [(d_gate.T.astype(BF16), wg), (d_up.T.astype(BF16), wu)])
    reduce_y(0)
    sw[...] = dot((hidden * value).T, member, ((1,), (0,)), exact)
    each(0, n_ep - 1, lambda i: s_send(i).start())
    rw[p] = sw[rows_at(here, rows)]
    reduce_core(1)
    reduce_x(0)
    fr[rows_at(p, PACK)] = fs[rows_at(p, PACK)]
    taken(fr.at[pl.ds(0, (n_ep - 1) * PACK)], r_f)
    slot_ids = lax.broadcasted_iota(jnp.int32, (n_ep * PACK, LANES), 1).astype(F32) + 1.0
    chosen = jnp.where(fr[:, 3 * count :].astype(F32) == slot_ids, 1.0, 0.0)
    placing = chosen.T.astype(BF16)[:slots]
    placed[...] = dot(placing, fr[:, : 3 * count], ((1,), (0,))).astype(BF16)
    for a in range(2):
        fetched = pl.ds(0, quarter + (n_y - 1) * side)
        taken(bufs[a].at[pl.ds(0, (n_z - 1) * rows), fetched], s_z.at[a])
        taken(bufs[a].at[pl.ds(0, n_z * (n_x - 1) * rows), fetched], s_x.at[a])
        taken(bufs[a].at[pl.ds(0, count - rows), pl.ds(0, (n_y - 1) * (quarter - side))], s_y.at[a])
        taken(bufs[a].at[pl.ds(0, count - rows), pl.ds(0, n_y * quarter)], s_c.at[a])
    taken(wa.at[pl.ds(0, count - rows)], s_w)
    taken(fs.at[pl.ds(0, (n_ep - 1) * PACK)], s_f)
    taken(sw.at[pl.ds(0, count - rows)], s_s)
    reduce_y(1)
    taken(rw.at[pl.ds(0, n_ep - 1)], r_s)
    rv[t] = jnp.sum(rw[...], 0)
    each(0, n_tp - 1, lambda i: v_send(i).start())
    reduce_x(1)
    reduce_z(0, out)

    taken(rv.at[pl.ds(0, n_tp - 1)], r_v)
    per_expert = jnp.sum(rv[...], 0)
    choice = lax.broadcasted_iota(jnp.int32, (rows, top), 1)
    picked = jnp.zeros((rows, top), F32)
    for k in range(top):
        value_k = jnp.sum(jnp.where(chosen_by[:, k : k + 1] == experts, per_expert, 0.0), 1, keepdims=True)
        picked = picked + jnp.where(choice == k, value_k, 0.0)
    dwt[...] = picked.T
    reduce_z(1, dtok)
    for store in stores:
        store.wait()
    taken(rv.at[pl.ds(0, n_tp - 1)], s_v)
    for a in range(2):
        taken(part.at[a, pl.ds(0, n_y)], s_rc.at[a])
        taken(part.at[a, pl.ds(0, n_y - 1)], s_ry.at[a])
        taken(part.at[a, 0, pl.ds(0, (n_x - 1) * group)], s_rx.at[a])
        taken(part.at[a, 0, pl.ds(0, (n_z - 1) * rows)], s_rz.at[a])


def gradients(out, dtok, dwt, placed, x, c, out_to, dtok_to, dwt_to, grad_gate, grad_up, grad_down):
    count = x.shape[0]

    @pl.when(pl.program_id(0) == 0)
    def hand_on():
        out_to[...] = out[...]
        dtok_to[...] = dtok[...]
        dwt_to[...] = dwt[...]

    for index, wide, grad in ((1, x, grad_gate), (2, x, grad_up), (0, c, grad_down)):
        factor = placed[:, index * count : (index + 1) * count]
        grad[...] = dot(factor, wide[...], ((1,), (0,))).astype(BF16)


def body(tokens, cotangent, w_gate, w_up, w_down, neuron_expert, neuron_slot, choice_expert, choice_weight):
    n_ep, n_tp = lax.axis_size("ep"), lax.axis_size("tp")
    n_y, n_z, n_x = grid_of(n_tp, n_ep)
    neurons, width = w_gate.shape
    rows = tokens.shape[0]
    count = n_ep * rows
    quarter = width // n_tp
    group = n_z * rows
    peer_slots = 2 * ((neurons + n_ep - 1) // n_ep)
    capacity = n_ep * peer_slots // E_DEV
    slots = E_DEV * capacity
    assert peer_slots <= PACK and slots <= LANES and E_DEV * n_ep <= LANES

    vmem = pl.BlockSpec(memory_space=pltpu.VMEM)
    anywhere = pl.BlockSpec(memory_space=pl.ANY)
    dma = pltpu.SemaphoreType.DMA
    small = jax.ShapeDtypeStruct((rows, quarter), BF16)
    grad = jax.ShapeDtypeStruct((slots, width), BF16)
    wide = jax.ShapeDtypeStruct((count, width), BF16)
    direct = (small, small, jax.ShapeDtypeStruct(choice_weight.shape[::-1], F32))
    results = pl.pallas_call(
        functools.partial(kernel, n_tp, n_ep),
        out_shape=direct + (jax.ShapeDtypeStruct((slots, 3 * count), BF16), wide, wide),
        in_specs=[vmem] * 9,
        out_specs=[vmem] * 4 + [anywhere] * 2,
        scratch_shapes=[
            pltpu.VMEM((count, width), BF16),
            pltpu.VMEM((count, width), BF16),
            pltpu.VMEM((count, LANES), F32),
            pltpu.VMEM((n_ep * PACK, 3 * count + LANES), BF16),
            pltpu.VMEM((n_ep * PACK, 3 * count + LANES), BF16),
            pltpu.VMEM((count, LANES), F32),
            pltpu.VMEM((n_ep, rows, LANES), F32),
            pltpu.VMEM((n_tp, rows, LANES), F32),
            pltpu.VMEM((2, n_tp, count, quarter), BF16),
            pltpu.VMEM((2, n_y, n_x, group, quarter), BF16),
            pltpu.VMEM((2, n_y - 1, n_x, group, quarter), BF16),
            pltpu.VMEM((2, n_x, group, quarter), BF16),
            pltpu.VMEM((2, n_z, rows, quarter), BF16),
            dma((2,)),
            dma((2,)),
            dma((2,)),
            dma((2,)),
            dma((2, n_ep, n_tp)),
            dma((2, n_ep, n_tp)),
            dma((2,)),
        ]
        + [dma] * 8
        + [
            dma((2,)),
            dma((2, n_y, n_x)),
            dma((2,)),
            dma((2, n_y, n_x)),
            dma((2,)),
            dma((2, n_x)),
            dma((2,)),
            dma((2, n_z)),
            dma((2,)),
        ],
        compiler_params=pltpu.CompilerParams(
            collective_id=0, has_side_effects=True, vmem_limit_bytes=62 * 1024 * 1024
        ),
    )(
        tokens, cotangent, w_gate, w_up, w_down,
        neuron_expert.reshape(1, -1), neuron_slot.reshape(1, -1), choice_expert.T, choice_weight.T,
    )
    chunk = min(width, 8 * LANES)

    def whole(ref):
        return pl.BlockSpec(ref.shape, lambda j: (0, 0))

    def columns(height):
        return pl.BlockSpec((height, chunk), lambda j: (0, j))

    output, d_tokens, d_weight, d_gate, d_up, d_down = pl.pallas_call(
        gradients,
        grid=(width // chunk,),
        out_shape=direct + (grad, grad, grad),
        in_specs=[whole(ref) for ref in results[:4]] + [columns(count)] * 2,
        out_specs=[whole(ref) for ref in direct] + [columns(slots)] * 3,
        compiler_params=pltpu.CompilerParams(vmem_limit_bytes=62 * 1024 * 1024),
    )(*results)
    d_weight = d_weight.T

    def expert_blocks(rows_):
        return rows_.reshape(E_DEV, capacity, width)

    return output, d_tokens, d_weight, expert_blocks(d_gate), expert_blocks(d_up), expert_blocks(d_down)


def solution(mesh):
    in_specs = (
        P("ep", None),
        P("ep", None),
        P(("tp", "ep"), None),
        P(("tp", "ep"), None),
        P(("tp", "ep"), None),
        P(("tp", "ep")),
        P(("tp", "ep")),
        P("ep", None),
        P("ep", None),
    )
    out_specs = (
        P("ep", "tp"),
        P("ep", "tp"),
        P("ep", None),
        P("ep", "tp", None),
        P("ep", "tp", None),
        P("ep", "tp", None),
    )
    return jax.shard_map(body, mesh=mesh, in_specs=in_specs, out_specs=out_specs, check_vma=False)
```

```python
import functools

import jax
import jax.numpy as jnp
from jax import lax
from jax.experimental import pallas as pl
from jax.experimental.pallas import tpu as pltpu
from jax.sharding import PartitionSpec as P

E_DEV = 2
CORES = 2
LANES = 128
PACK = 16
MESH = pl.DeviceIdType.MESH
BF16, F32 = jnp.bfloat16, jnp.float32


def grid_of(n_tp, n_ep):
    n_x = 1
    while 8 * n_x * n_x <= n_ep:
        n_x *= 2
    return n_tp // CORES, n_ep // n_x, n_x


def each(low, high, step):
    def run(i, carry):
        step(i)
        return carry

    if high - low == 1:
        step(low)
    elif high > low:
        lax.fori_loop(low, high, run, 0)


def dot(left, right, dims, precision=None):
    return lax.dot_general(left, right, (dims, ((), ())), precision=precision, preferred_element_type=F32)


def kernel(
    n_tp, n_ep, tok, cot, wg, wu, wd, ne, ns, ce, cw,
    out, dtok, dwt, placed, x_out, c_out,
    xs, cs, wa, fs, fr, sw, rw, rv, part, shared, stack, crossing, ry, rx, rz,
    s_z, s_x, s_y, s_c, r_ag, r_sd, r_c, s_w, r_w, s_f, r_f, s_s, r_s, s_v, r_v,
    s_wt, r_wt, s_fx, r_fx, s_ry, r_ry, s_rx, r_rx, s_rz, r_rz, s_g,
):
    n_y, n_z, n_x = grid_of(n_tp, n_ep)
    t, p = lax.axis_index("tp"), lax.axis_index("ep")
    y, c = t // CORES, lax.rem(t, CORES)
    z, x = p // n_x, lax.rem(p, n_x)
    other = 1 - c
    rows, width = tok.shape
    count = n_ep * rows
    quarter = width // n_tp
    group = n_z * rows
    bufs = (xs, cs)

    def place(z_, x_):
        return x_ * n_z + z_

    def at(z_, x_):
        return (t, z_ * n_x + x_)

    def ep_peer(i):
        return lax.rem(p + 1 + i, n_ep)

    def place_of(p_):
        return place(p_ // n_x, lax.rem(p_, n_x))

    def copy(src, dst, send, recv, device):
        return pltpu.make_async_remote_copy(
            src_ref=src, dst_ref=dst, send_sem=send, recv_sem=recv, device_id=device, device_id_type=MESH
        )

    def got(dst, recv, device):
        copy(dst, dst, s_v, recv, device).wait_recv()

    def taken(ref, sem):
        pltpu.make_async_copy(ref, ref, sem).wait()

    here = place(z, x)

    def rows_at(i, size):
        return pl.ds(pl.multiple_of(i * size, size), size)

    def cols_at(q):
        return pl.ds(pl.multiple_of(q * quarter, LANES), quarter)

    side = quarter // 2

    def block(a, k, q):
        return bufs[a].at[rows_at(k, rows), cols_at(q)]

    def side_block(a, k, q):
        return bufs[a].at[rows_at(k, rows), pl.ds(pl.multiple_of(q * quarter, LANES), side)]

    def rest_block(a, k, q):
        return bufs[a].at[rows_at(k, rows), pl.ds(pl.multiple_of(q * quarter + side, LANES), quarter - side)]

    def ranked(k):
        return place(lax.rem(z + n_z - lax.rem(k, n_z), n_z), lax.rem(x + k // n_z, n_x))

    def next_y(i):
        return lax.rem(y + 1 + i, n_y)

    sibling = (y * CORES + other, p)

    def z_send(a, i):
        b = block(a, here, t)
        return copy(b, b, s_z.at[a], r_ag.at[a, here, t], at(lax.rem(z + 1 + i, n_z), x))

    def zs_send(a, i, j):
        q = next_y(j) * CORES + c
        b = side_block(a, here, q)
        return copy(b, b, s_z.at[a], r_sd.at[a, here, q], at(lax.rem(z + 1 + i, n_z), x))

    def x_send(a, k, i):
        b = block(a, ranked(k), t)
        return copy(b, b, s_x.at[a], r_ag.at[a, ranked(k), t], at(z, lax.rem(x + 1 + i, n_x)))

    def xs_send(a, k, i, j):
        q = next_y(j) * CORES + c
        b = side_block(a, ranked(k), q)
        return copy(b, b, s_x.at[a], r_sd.at[a, ranked(k), q], at(z, lax.rem(x + 1 + i, n_x)))

    def y_send(a, k, i):
        b = rest_block(a, ranked(k), t)
        return copy(b, b, s_y.at[a], r_ag.at[a, ranked(k), t], (next_y(i) * CORES + c, p))

    def c_send(a, k, qy):
        b = block(a, ranked(k), qy * CORES + c)
        return copy(b, b, s_c.at[a], r_c.at[a], sibling)

    def arrived(a, k, q):
        got(block(a, ranked(k), q), r_ag.at[a, ranked(k), q], sibling)

    def side_arrived(a, k, q):
        got(side_block(a, ranked(k), q), r_sd.at[a, ranked(k), q], sibling)

    def rest_arrived(a, k, q):
        got(rest_block(a, ranked(k), q), r_ag.at[a, ranked(k), q], sibling)

    def w_send(i):
        b = wa.at[rows_at(here, rows)]
        return copy(b, b, s_w, r_w, (t, ep_peer(i)))

    def f_send(i):
        to = ep_peer(i)
        return copy(fs.at[rows_at(to, PACK)], fr.at[rows_at(p, PACK)], s_f, r_f, (t, to))

    def s_send(i):
        to = ep_peer(i)
        return copy(sw.at[rows_at(place_of(to), rows)], rw.at[p], s_s, r_s, (t, to))

    def v_send(i):
        to = lax.rem(t + 1 + i, n_tp)
        return copy(rv.at[t], rv.at[t], s_v, r_v, (to, p))

    high = shared.shape[1] // 3

    def wt_send(qy, w):
        src = shared.at[qy, pl.ds(w * high, high)]
        dst = stack.at[qy, rows_at(w * CORES + c, high)]
        return copy(src, dst, s_wt, r_wt, sibling)

    def fx_send(w):
        ref = crossing.at[rows_at(w * CORES + c, high)]
        return copy(ref, ref, s_fx.at[w], r_fx.at[w], sibling)

    def ry_send(a, i, g):
        to = next_y(i) * CORES + c
        src = part.at[a, next_y(i), rows_at(g, group)]
        return copy(src, ry.at[a, n_y - 2 - i, g], s_ry.at[a], r_ry.at[a, n_y - 2 - i, g], (to, p))

    def rx_send(a, i):
        to = lax.rem(x + 1 + i, n_x)
        src = part.at[a, y, rows_at(to, group)]
        return copy(src, rx.at[a, x], s_rx.at[a], r_rx.at[a, x], at(z, to))

    def rz_send(a, i):
        to = lax.rem(z + 1 + i, n_z)
        src = part.at[a, y, rows_at(place(to, x), rows)]
        return copy(src, rz.at[a, z], s_rz.at[a], r_rz.at[a, z], at(to, x))

    barrier = pltpu.get_barrier_semaphore()
    each(0, n_ep - 1, lambda i: pl.semaphore_signal(barrier, inc=1, device_id=(t, ep_peer(i)), device_id_type=MESH))
    each(
        0, n_tp - 1,
        lambda i: pl.semaphore_signal(barrier, inc=1, device_id=(lax.rem(t + 1 + i, n_tp), p), device_id_type=MESH),
    )
    xs[rows_at(here, rows)] = tok[...]
    cs[rows_at(here, rows)] = cot[...]
    pl.semaphore_wait(barrier, n_ep - 1 + n_tp - 1)

    for a in range(2):
        each(0, n_z - 1, lambda i: z_send(a, i).start())
        each(0, n_x - 1, lambda i: x_send(a, 0, i).start())
        each(0, n_z - 1, lambda i: each(0, n_y - 1, lambda j: zs_send(a, i, j).start()))
        each(0, n_x - 1, lambda i: each(0, n_y - 1, lambda j: xs_send(a, 0, i, j).start()))

    held = wg.shape[0]
    blank = jnp.zeros((high - held, quarter), BF16)
    for w, weight in enumerate((wd, wg, wu)):

        def lay(qy):
            shared[qy, w * high : w * high + held] = weight[:, cols_at(qy * CORES + other)]
            shared[qy, w * high + held : (w + 1) * high] = blank
            wt_send(qy, w).start()
            own = pl.multiple_of((w * CORES + c) * high, high)
            stack[qy, pl.ds(own, high)] = jnp.concatenate([weight[:, cols_at(qy * CORES + c)], blank], 0)

        each(0, n_y, lay)
    experts = lax.broadcasted_iota(jnp.int32, (rows, LANES), 1).astype(F32)
    by_expert = jnp.zeros((rows, LANES), F32)
    chosen_by, weight_by = ce[...].astype(F32).T, cw[...].T
    top = ce.shape[0]
    for k in range(top):
        by_expert = by_expert + jnp.where(chosen_by[:, k : k + 1] == experts, weight_by[:, k : k + 1], 0.0)
    wa[rows_at(here, rows)] = by_expert
    each(0, n_ep - 1, lambda i: w_send(i).start())

    neurons = wg.shape[0]
    slots = placed.shape[0] // 3
    named = ne[...]
    owner = lax.div(named, E_DEV)

    def ids(size):
        return lax.broadcasted_iota(jnp.int32, (size, neurons), 0)

    def ones(mask):
        return jnp.where(mask, 1.0, 0.0)

    member = ones(ids(LANES) == named).T
    owned = ones(ids(n_ep) == owner)
    order = ones(ids(neurons) < lax.broadcasted_iota(jnp.int32, (neurons, neurons), 1))
    before = dot(owned.astype(BF16), order.astype(BF16), ((1,), (0,)))
    target = owner.astype(F32) * PACK + jnp.sum(owned * before, 0, keepdims=True)
    pack = ones(ids(n_ep * PACK).astype(F32) == target).astype(BF16)
    label = (lax.rem(named, E_DEV) * (slots // E_DEV) + ns[...] + 1).astype(F32)
    label = jnp.broadcast_to(label, (LANES, neurons)).T.astype(BF16)

    def forward(a, k, near):
        arrived(a, k, t)
        if near:
            each(0, n_x - 1, lambda i: x_send(a, k, i).start())
        each(0, n_y - 1, lambda i: y_send(a, k, i).start())
        c_send(a, k, y).start()

        def one(j):
            side_arrived(a, k, next_y(j) * CORES + c)
            if near:
                each(0, n_x - 1, lambda i: xs_send(a, k, i, j).start())

        each(0, n_y - 1, one)

    def across(a, k):
        def one(i):
            rest_arrived(a, k, next_y(i) * CORES + c)
            c_send(a, k, next_y(i)).start()

        each(0, n_y - 1, one)

    def project(a, weights):
        def add(q, totals):
            wide = bufs[a][:, cols_at(q)]
            return tuple(total + dot(weight[:, cols_at(q)], wide, ((1,), (1,))) for total, weight in zip(totals, weights))

        def mine(i, totals):
            return add(lax.rem(y + i, n_y) * CORES + c, totals)

        def theirs(i, totals):
            return add(lax.rem(y + i, n_y) * CORES + other, totals)

        totals = tuple(jnp.zeros((neurons, count), F32) for _ in weights)
        totals = lax.fori_loop(0, n_y, mine, totals)
        taken(bufs[a].at[pl.ds(0, count - rows), pl.ds(0, n_y * quarter)], r_c.at[a])
        return lax.fori_loop(0, n_y, theirs, totals)

    step_cols = min(quarter, 512)

    def hand(w, factor):
        pad = jnp.zeros((high - neurons, count), F32)
        crossing[rows_at(w * CORES + c, high)] = jnp.concatenate([factor, pad], 0)
        fx_send(w).start()

    def spread(a, low, tall):
        for w in range(low, low + tall):
            got(crossing.at[rows_at(w * CORES + other, high)], r_fx.at[w], sibling)
        span = slice(low * CORES * high, (low + tall) * CORES * high)
        factor = crossing[span].T.astype(BF16)

        def one(qy):
            def chunk(j):
                at_cols = pl.ds(pl.multiple_of(j * step_cols, LANES), step_cols)
                part[a, qy, :, at_cols] = dot(factor, stack[qy, span, at_cols], ((1,), (0,))).astype(BF16)

            each(0, quarter // step_cols, chunk)

        def away(i):
            one(next_y(i))
            each(0, n_x, lambda g: ry_send(a, i, lax.rem(x + 1 + g, n_x)).start())

        each(0, n_y - 1, away)
        one(y)

    def add_into(a, q, base, ref):
        def some(j):
            span = rows_at(base + j, rows)
            part[a, q, span] = (
                part[a, q, span].astype(F32) + ref[rows_at(j, rows)].astype(F32)
            ).astype(BF16)

        each(0, ref.shape[0] // rows, some)

    def reduce_y(a):
        def one(g):
            def add(i):
                qy = lax.rem(y + 1 + i, n_y)
                got(ry.at[a, i, g], r_ry.at[a, i, g], (qy * CORES + c, p))
                add_into(a, y, g * n_z, ry.at[a, i, g])

            each(0, n_y - 1, add)

        def send(i):
            one(lax.rem(x + 1 + i, n_x))
            rx_send(a, i).start()

        each(0, n_x - 1, send)
        one(x)

    def reduce_x(a):
        def add(i):
            from_x = lax.rem(x + 1 + i, n_x)
            got(rx.at[a, from_x], r_rx.at[a, from_x], at(z, from_x))
            add_into(a, y, x * n_z, rx.at[a, from_x])

        each(0, n_x - 1, add)
        each(0, n_z - 1, lambda i: rz_send(a, i).start())

    def reduce_z(a, result):
        total = part[a, y, rows_at(here, rows)].astype(F32)
        for i in range(n_z - 1):
            from_z = lax.rem(z + 1 + i, n_z)
            got(rz.at[a, from_z], r_rz.at[a, from_z], at(from_z, x))
            total = total + rz[a, from_z].astype(F32)
        result[...] = total.astype(BF16)

    exact = lax.Precision.HIGHEST
    each(1, n_z, lambda k: forward(0, k, True))
    each(n_z, n_ep, lambda k: forward(0, k, False))

    def both(k, near):
        across(0, k)
        forward(1, k, near)

    each(1, n_z, lambda k: both(k, True))
    each(n_z, n_ep, lambda k: both(k, False))
    gate, upper = project(0, (wg, wu))
    stores = [pltpu.make_async_copy(buf, ref, s_g.at[i]) for i, (buf, ref) in enumerate(((xs, x_out), (cs, c_out)))]
    stores[0].start()
    taken(wa.at[pl.ds(0, count - rows)], r_w)
    weight = dot(member, wa[...], ((1,), (1,)), exact)
    sig = 1.0 / (1.0 + jnp.exp(-gate))
    silu = gate * sig
    hidden = silu * upper
    scaled = weight * hidden
    hand(0, scaled)
    each(1, n_ep, lambda k: across(1, k))
    taken(stack.at[pl.ds(0, n_y), pl.ds(0, 3 * high)], r_wt)
    spread(0, 0, 1)
    (value,) = project(1, (wd,))
    stores[1].start()
    d_hidden = weight * value
    d_gate = d_hidden * upper * (sig * (1.0 + gate * (1.0 - sig)))
    d_up = d_hidden * silu
    hand(1, d_gate)
    hand(2, d_up)
    factors = jnp.concatenate([scaled.astype(BF16), d_gate.astype(BF16), d_up.astype(BF16), label], 1)
    fs[...] = dot(pack, factors, ((1,), (0,))).astype(BF16)
    each(0, n_ep - 1, lambda i: f_send(i).start())
    spread(1, 1, 2)
    reduce_y(0)
    sw[...] = dot((hidden * value).T, member, ((1,), (0,)), exact)
    each(0, n_ep - 1, lambda i: s_send(i).start())
    rw[p] = sw[rows_at(here, rows)]
    reduce_x(0)
    fr[rows_at(p, PACK)] = fs[rows_at(p, PACK)]
    taken(fr.at[pl.ds(0, (n_ep - 1) * PACK)], r_f)
    slot_ids = lax.broadcasted_iota(jnp.int32, (n_ep * PACK, LANES), 1).astype(F32) + 1.0
    chosen = jnp.where(fr[:, 3 * count :].astype(F32) == slot_ids, 1.0, 0.0)
    placing = chosen.T.astype(BF16)[:slots]
    for i in range(3):
        placed[i * slots : (i + 1) * slots] = dot(placing, fr[:, i * count : (i + 1) * count], ((1,), (0,))).astype(BF16)
    for a in range(2):
        fetched = pl.ds(0, quarter + (n_y - 1) * side)
        taken(bufs[a].at[pl.ds(0, (n_z - 1) * rows), fetched], s_z.at[a])
        taken(bufs[a].at[pl.ds(0, n_z * (n_x - 1) * rows), fetched], s_x.at[a])
        taken(bufs[a].at[pl.ds(0, count - rows), pl.ds(0, (n_y - 1) * (quarter - side))], s_y.at[a])
        taken(bufs[a].at[pl.ds(0, count - rows), pl.ds(0, n_y * quarter)], s_c.at[a])
    taken(wa.at[pl.ds(0, count - rows)], s_w)
    taken(fs.at[pl.ds(0, (n_ep - 1) * PACK)], s_f)
    taken(sw.at[pl.ds(0, count - rows)], s_s)
    reduce_y(1)
    taken(rw.at[pl.ds(0, n_ep - 1)], r_s)
    rv[t] = jnp.sum(rw[...], 0)
    each(0, n_tp - 1, lambda i: v_send(i).start())
    reduce_x(1)
    reduce_z(0, out)

    taken(rv.at[pl.ds(0, n_tp - 1)], r_v)
    per_expert = jnp.sum(rv[...], 0)
    choice = lax.broadcasted_iota(jnp.int32, (rows, top), 1)
    picked = jnp.zeros((rows, top), F32)
    for k in range(top):
        value_k = jnp.sum(jnp.where(chosen_by[:, k : k + 1] == experts, per_expert, 0.0), 1, keepdims=True)
        picked = picked + jnp.where(choice == k, value_k, 0.0)
    dwt[...] = picked.T
    reduce_z(1, dtok)
    for store in stores:
        store.wait()
    taken(rv.at[pl.ds(0, n_tp - 1)], s_v)
    for a in range(2):
        taken(part.at[a, pl.ds(0, n_y - 1)], s_ry.at[a])
        taken(part.at[a, 0, pl.ds(0, (n_x - 1) * group)], s_rx.at[a])
        taken(part.at[a, 0, pl.ds(0, (n_z - 1) * rows)], s_rz.at[a])
    for w in range(3):
        taken(crossing.at[pl.ds(0, high)], s_fx.at[w])
    taken(shared, s_wt)


def gradients(out, dtok, dwt, placed, x, c, out_to, dtok_to, dwt_to, grad_gate, grad_up, grad_down):
    @pl.when(pl.program_id(0) == 0)
    def hand_on():
        out_to[...] = out[...]
        dtok_to[...] = dtok[...]
        dwt_to[...] = dwt[...]

    slots = grad_down.shape[0]
    grad_down[...] = dot(placed[:slots], c[...], ((1,), (0,))).astype(BF16)
    both = dot(placed[slots:], x[...], ((1,), (0,))).astype(BF16)
    grad_gate[...] = both[:slots]
    grad_up[...] = both[slots:]


def body(tokens, cotangent, w_gate, w_up, w_down, neuron_expert, neuron_slot, choice_expert, choice_weight):
    n_ep, n_tp = lax.axis_size("ep"), lax.axis_size("tp")
    n_y, n_z, n_x = grid_of(n_tp, n_ep)
    neurons, width = w_gate.shape
    rows = tokens.shape[0]
    count = n_ep * rows
    quarter = width // n_tp
    group = n_z * rows
    high = -(-neurons // PACK) * PACK
    peer_slots = 2 * ((neurons + n_ep - 1) // n_ep)
    capacity = n_ep * peer_slots // E_DEV
    slots = E_DEV * capacity
    assert peer_slots <= PACK and slots <= LANES and E_DEV * n_ep <= LANES

    vmem = pl.BlockSpec(memory_space=pltpu.VMEM)
    anywhere = pl.BlockSpec(memory_space=pl.ANY)
    dma = pltpu.SemaphoreType.DMA
    small = jax.ShapeDtypeStruct((rows, quarter), BF16)
    grad = jax.ShapeDtypeStruct((slots, width), BF16)
    wide = jax.ShapeDtypeStruct((count, width), BF16)
    direct = (small, small, jax.ShapeDtypeStruct(choice_weight.shape[::-1], F32))
    results = pl.pallas_call(
        functools.partial(kernel, n_tp, n_ep),
        out_shape=direct + (jax.ShapeDtypeStruct((3 * slots, count), BF16), wide, wide),
        in_specs=[vmem] * 9,
        out_specs=[vmem] * 4 + [anywhere] * 2,
        scratch_shapes=[
            pltpu.VMEM((count, width), BF16),
            pltpu.VMEM((count, width), BF16),
            pltpu.VMEM((count, LANES), F32),
            pltpu.VMEM((n_ep * PACK, 3 * count + LANES), BF16),
            pltpu.VMEM((n_ep * PACK, 3 * count + LANES), BF16),
            pltpu.VMEM((count, LANES), F32),
            pltpu.VMEM((n_ep, rows, LANES), F32),
            pltpu.VMEM((n_tp, rows, LANES), F32),
            pltpu.VMEM((2, n_y, count, quarter), BF16),
            pltpu.VMEM((n_y, 3 * high, quarter), BF16),
            pltpu.VMEM((n_y, 3 * CORES * high, quarter), BF16),
            pltpu.VMEM((3 * CORES * high, count), F32),
            pltpu.VMEM((2, n_y - 1, n_x, group, quarter), BF16),
            pltpu.VMEM((2, n_x, group, quarter), BF16),
            pltpu.VMEM((2, n_z, rows, quarter), BF16),
            dma((2,)),
            dma((2,)),
            dma((2,)),
            dma((2,)),
            dma((2, n_ep, n_tp)),
            dma((2, n_ep, n_tp)),
            dma((2,)),
        ]
        + [dma] * 8
        + [
            dma,
            dma,
            dma((3,)),
            dma((3,)),
            dma((2,)),
            dma((2, n_y, n_x)),
            dma((2,)),
            dma((2, n_x)),
            dma((2,)),
            dma((2, n_z)),
            dma((2,)),
        ],
        compiler_params=pltpu.CompilerParams(
            collective_id=0, has_side_effects=True, vmem_limit_bytes=62 * 1024 * 1024
        ),
    )(
        tokens, cotangent, w_gate, w_up, w_down,
        neuron_expert.reshape(1, -1), neuron_slot.reshape(1, -1), choice_expert.T, choice_weight.T,
    )
    chunk = min(width, 16 * LANES)

    def whole(ref):
        return pl.BlockSpec(ref.shape, lambda j: (0, 0))

    def columns(height):
        return pl.BlockSpec((height, chunk), lambda j: (0, j))

    output, d_tokens, d_weight, d_gate, d_up, d_down = pl.pallas_call(
        gradients,
        grid=(width // chunk,),
        out_shape=direct + (grad, grad, grad),
        in_specs=[whole(ref) for ref in results[:4]] + [columns(count)] * 2,
        out_specs=[whole(ref) for ref in direct] + [columns(slots)] * 3,
        compiler_params=pltpu.CompilerParams(vmem_limit_bytes=62 * 1024 * 1024),
    )(*results)
    d_weight = d_weight.T

    def expert_blocks(rows_):
        return rows_.reshape(E_DEV, capacity, width)

    return output, d_tokens, d_weight, expert_blocks(d_gate), expert_blocks(d_up), expert_blocks(d_down)


def solution(mesh):
    in_specs = (
        P("ep", None),
        P("ep", None),
        P(("tp", "ep"), None),
        P(("tp", "ep"), None),
        P(("tp", "ep"), None),
        P(("tp", "ep")),
        P(("tp", "ep")),
        P("ep", None),
        P("ep", None),
    )
    out_specs = (
        P("ep", "tp"),
        P("ep", "tp"),
        P("ep", None),
        P("ep", "tp", None),
        P("ep", "tp", None),
        P("ep", "tp", None),
    )
    return jax.shard_map(body, mesh=mesh, in_specs=in_specs, out_specs=out_specs, check_vma=False)
```

```python
import functools

import jax
import jax.numpy as jnp
from jax import lax
from jax.experimental import pallas as pl
from jax.experimental.pallas import tpu as pltpu
from jax.sharding import PartitionSpec as P

E_DEV = 2
CORES = 2
LANES = 128
PACK = 16
MESH = pl.DeviceIdType.MESH
BF16, F32 = jnp.bfloat16, jnp.float32


def grid_of(n_tp, n_ep):
    n_x = 1
    while 8 * n_x * n_x <= n_ep:
        n_x *= 2
    return n_tp // CORES, n_ep // n_x, n_x


def each(low, high, step):
    def run(i, carry):
        step(i)
        return carry

    if high - low == 1:
        step(low)
    elif high > low:
        lax.fori_loop(low, high, run, 0)


def dot(left, right, dims, precision=None):
    return lax.dot_general(left, right, (dims, ((), ())), precision=precision, preferred_element_type=F32)


def kernel(
    n_tp, n_ep, tok, cot, wg, wu, wd, ne, ns, ce, cw,
    out, dtok, dwt, placed, x_out, c_out,
    xs, cs, wa, fs, fr, sw, rw, rv, part, shared, stack, crossing, ry, rx, rz,
    s_z, s_x, s_y, s_c, r_ag, r_sd, r_c, s_w, r_w, s_f, r_f, s_s, r_s, s_v, r_v,
    s_wt, r_wt, s_fx, r_fx, s_ry, r_ry, s_rx, r_rx, s_rz, r_rz, s_g,
):
    n_y, n_z, n_x = grid_of(n_tp, n_ep)
    t, p = lax.axis_index("tp"), lax.axis_index("ep")
    y, c = t // CORES, lax.rem(t, CORES)
    z, x = p // n_x, lax.rem(p, n_x)
    other = 1 - c
    rows, width = tok.shape
    count = n_ep * rows
    quarter = width // n_tp
    group = n_z * rows
    bufs = (xs, cs)

    def place(z_, x_):
        return x_ * n_z + z_

    def at(z_, x_):
        return (t, z_ * n_x + x_)

    def ep_peer(i):
        return lax.rem(p + 1 + i, n_ep)

    def place_of(p_):
        return place(p_ // n_x, lax.rem(p_, n_x))

    def copy(src, dst, send, recv, device):
        return pltpu.make_async_remote_copy(
            src_ref=src, dst_ref=dst, send_sem=send, recv_sem=recv, device_id=device, device_id_type=MESH
        )

    def got(dst, recv, device):
        copy(dst, dst, s_v, recv, device).wait_recv()

    def taken(ref, sem):
        pltpu.make_async_copy(ref, ref, sem).wait()

    here = place(z, x)

    def rows_at(i, size):
        return pl.ds(pl.multiple_of(i * size, size), size)

    def cols_at(q):
        return pl.ds(pl.multiple_of(q * quarter, LANES), quarter)

    side = quarter // 2

    def block(a, k, q):
        return bufs[a].at[rows_at(k, rows), cols_at(q)]

    def side_block(a, k, q):
        return bufs[a].at[rows_at(k, rows), pl.ds(pl.multiple_of(q * quarter, LANES), side)]

    def rest_block(a, k, q):
        return bufs[a].at[rows_at(k, rows), pl.ds(pl.multiple_of(q * quarter + side, LANES), quarter - side)]

    def ranked(k):
        return place(lax.rem(z + n_z - lax.rem(k, n_z), n_z), lax.rem(x + k // n_z, n_x))

    def next_y(i):
        return lax.rem(y + 1 + i, n_y)

    sibling = (y * CORES + other, p)

    def z_send(a, i):
        b = block(a, here, t)
        return copy(b, b, s_z.at[a], r_ag.at[a, here, t], at(lax.rem(z + 1 + i, n_z), x))

    def zs_send(a, i, j):
        q = next_y(j) * CORES + c
        b = side_block(a, here, q)
        return copy(b, b, s_z.at[a], r_sd.at[a, here, q], at(lax.rem(z + 1 + i, n_z), x))

    def x_send(a, k, i):
        b = block(a, ranked(k), t)
        return copy(b, b, s_x.at[a], r_ag.at[a, ranked(k), t], at(z, lax.rem(x + 1 + i, n_x)))

    def xs_send(a, k, i, j):
        q = next_y(j) * CORES + c
        b = side_block(a, ranked(k), q)
        return copy(b, b, s_x.at[a], r_sd.at[a, ranked(k), q], at(z, lax.rem(x + 1 + i, n_x)))

    def y_send(a, k, i):
        b = rest_block(a, ranked(k), t)
        return copy(b, b, s_y.at[a], r_ag.at[a, ranked(k), t], (next_y(i) * CORES + c, p))

    def c_send(a, k, qy):
        b = block(a, ranked(k), qy * CORES + c)
        return copy(b, b, s_c.at[a], r_c.at[a], sibling)

    def arrived(a, k, q):
        got(block(a, ranked(k), q), r_ag.at[a, ranked(k), q], sibling)

    def side_arrived(a, k, q):
        got(side_block(a, ranked(k), q), r_sd.at[a, ranked(k), q], sibling)

    def rest_arrived(a, k, q):
        got(rest_block(a, ranked(k), q), r_ag.at[a, ranked(k), q], sibling)

    def w_send(i):
        b = wa.at[rows_at(here, rows)]
        return copy(b, b, s_w, r_w, (t, ep_peer(i)))

    def f_send(i):
        to = ep_peer(i)
        return copy(fs.at[rows_at(to, PACK)], fr.at[rows_at(p, PACK)], s_f, r_f, (t, to))

    def s_send(i):
        to = ep_peer(i)
        return copy(sw.at[rows_at(place_of(to), rows)], rw.at[p], s_s, r_s, (t, to))

    def v_send(i):
        to = lax.rem(t + 1 + i, n_tp)
        return copy(rv.at[t], rv.at[t], s_v, r_v, (to, p))

    high = shared.shape[1] // 3

    def wt_send(qy, w):
        src = shared.at[qy, pl.ds(w * high, high)]
        dst = stack.at[qy, rows_at(w * CORES + c, high)]
        return copy(src, dst, s_wt, r_wt, sibling)

    def fx_send(w):
        ref = crossing.at[rows_at(w * CORES + c, high)]
        return copy(ref, ref, s_fx.at[w], r_fx.at[w], sibling)

    def ry_send(a, i, g):
        to = next_y(i) * CORES + c
        src = part.at[a, next_y(i), rows_at(g, group)]
        return copy(src, ry.at[a, n_y - 2 - i, g], s_ry.at[a], r_ry.at[a, n_y - 2 - i, g], (to, p))

    def rx_send(a, i):
        to = lax.rem(x + 1 + i, n_x)
        src = part.at[a, y, rows_at(to, group)]
        return copy(src, rx.at[a, x], s_rx.at[a], r_rx.at[a, x], at(z, to))

    def rz_send(a, i):
        to = lax.rem(z + 1 + i, n_z)
        src = part.at[a, y, rows_at(place(to, x), rows)]
        return copy(src, rz.at[a, z], s_rz.at[a], r_rz.at[a, z], at(to, x))

    barrier = pltpu.get_barrier_semaphore()
    each(0, n_ep - 1, lambda i: pl.semaphore_signal(barrier, inc=1, device_id=(t, ep_peer(i)), device_id_type=MESH))
    each(
        0, n_tp - 1,
        lambda i: pl.semaphore_signal(barrier, inc=1, device_id=(lax.rem(t + 1 + i, n_tp), p), device_id_type=MESH),
    )
    xs[rows_at(here, rows)] = tok[...]
    cs[rows_at(here, rows)] = cot[...]
    pl.semaphore_wait(barrier, n_ep - 1 + n_tp - 1)

    def open_with(a):
        each(0, n_z - 1, lambda i: z_send(a, i).start())
        each(0, n_x - 1, lambda i: x_send(a, 0, i).start())
        each(0, n_z - 1, lambda i: each(0, n_y - 1, lambda j: zs_send(a, i, j).start()))
        each(0, n_x - 1, lambda i: each(0, n_y - 1, lambda j: xs_send(a, 0, i, j).start()))

    open_with(0)

    held = wg.shape[0]
    blank = jnp.zeros((high - held, quarter), BF16)
    for w, weight in enumerate((wd, wg, wu)):

        def lay(qy):
            shared[qy, w * high : w * high + held] = weight[:, cols_at(qy * CORES + other)]
            shared[qy, w * high + held : (w + 1) * high] = blank
            wt_send(qy, w).start()
            own = pl.multiple_of((w * CORES + c) * high, high)
            stack[qy, pl.ds(own, high)] = jnp.concatenate([weight[:, cols_at(qy * CORES + c)], blank], 0)

        each(0, n_y, lay)
    experts = lax.broadcasted_iota(jnp.int32, (rows, LANES), 1).astype(F32)
    by_expert = jnp.zeros((rows, LANES), F32)
    chosen_by, weight_by = ce[...].astype(F32).T, cw[...].T
    top = ce.shape[0]
    for k in range(top):
        by_expert = by_expert + jnp.where(chosen_by[:, k : k + 1] == experts, weight_by[:, k : k + 1], 0.0)
    wa[rows_at(here, rows)] = by_expert
    each(0, n_ep - 1, lambda i: w_send(i).start())

    neurons = wg.shape[0]
    slots = placed.shape[0] // 3
    named = ne[...]
    owner = lax.div(named, E_DEV)

    def ids(size):
        return lax.broadcasted_iota(jnp.int32, (size, neurons), 0)

    def ones(mask):
        return jnp.where(mask, 1.0, 0.0)

    member = ones(ids(LANES) == named).T
    owned = ones(ids(n_ep) == owner)
    order = ones(ids(neurons) < lax.broadcasted_iota(jnp.int32, (neurons, neurons), 1))
    before = dot(owned.astype(BF16), order.astype(BF16), ((1,), (0,)))
    target = owner.astype(F32) * PACK + jnp.sum(owned * before, 0, keepdims=True)
    pack = ones(ids(n_ep * PACK).astype(F32) == target).astype(BF16)
    label = (lax.rem(named, E_DEV) * (slots // E_DEV) + ns[...] + 1).astype(F32)
    label = jnp.broadcast_to(label, (LANES, neurons)).T.astype(BF16)

    def forward(a, k, near):
        arrived(a, k, t)
        if near:
            each(0, n_x - 1, lambda i: x_send(a, k, i).start())
        each(0, n_y - 1, lambda i: y_send(a, k, i).start())
        c_send(a, k, y).start()

        def one(j):
            side_arrived(a, k, next_y(j) * CORES + c)
            if near:
                each(0, n_x - 1, lambda i: xs_send(a, k, i, j).start())

        each(0, n_y - 1, one)

    def across(a, k):
        def one(i):
            rest_arrived(a, k, next_y(i) * CORES + c)
            c_send(a, k, next_y(i)).start()

        each(0, n_y - 1, one)

    def project(a, weights):
        def add(q, totals):
            wide = bufs[a][:, cols_at(q)]
            return tuple(total + dot(weight[:, cols_at(q)], wide, ((1,), (1,))) for total, weight in zip(totals, weights))

        def mine(i, totals):
            return add(lax.rem(y + i, n_y) * CORES + c, totals)

        def theirs(i, totals):
            return add(lax.rem(y + i, n_y) * CORES + other, totals)

        totals = tuple(jnp.zeros((neurons, count), F32) for _ in weights)
        totals = lax.fori_loop(0, n_y, mine, totals)
        taken(bufs[a].at[pl.ds(0, count - rows), pl.ds(0, n_y * quarter)], r_c.at[a])
        return lax.fori_loop(0, n_y, theirs, totals)

    step_cols = min(quarter, 512)

    def hand(w, factor):
        pad = jnp.zeros((high - neurons, count), F32)
        crossing[rows_at(w * CORES + c, high)] = jnp.concatenate([factor, pad], 0)
        fx_send(w).start()

    def spread(a, low, tall):
        for w in range(low, low + tall):
            got(crossing.at[rows_at(w * CORES + other, high)], r_fx.at[w], sibling)
        span = slice(low * CORES * high, (low + tall) * CORES * high)
        factor = crossing[span].T.astype(BF16)

        def one(qy):
            def chunk(j):
                at_cols = pl.ds(pl.multiple_of(j * step_cols, LANES), step_cols)
                part[a, qy, :, at_cols] = dot(factor, stack[qy, span, at_cols], ((1,), (0,))).astype(BF16)

            each(0, quarter // step_cols, chunk)

        def away(i):
            one(next_y(i))
            each(0, n_x, lambda g: ry_send(a, i, lax.rem(x + 1 + g, n_x)).start())

        each(0, n_y - 1, away)
        one(y)

    def add_into(a, q, base, ref):
        def some(j):
            span = rows_at(base + j, rows)
            part[a, q, span] = (
                part[a, q, span].astype(F32) + ref[rows_at(j, rows)].astype(F32)
            ).astype(BF16)

        each(0, ref.shape[0] // rows, some)

    def reduce_y(a):
        def one(g):
            def add(i):
                qy = lax.rem(y + 1 + i, n_y)
                got(ry.at[a, i, g], r_ry.at[a, i, g], (qy * CORES + c, p))
                add_into(a, y, g * n_z, ry.at[a, i, g])

            each(0, n_y - 1, add)

        def send(i):
            one(lax.rem(x + 1 + i, n_x))
            rx_send(a, i).start()

        each(0, n_x - 1, send)
        one(x)

    def reduce_x(a):
        def add(i):
            from_x = lax.rem(x + 1 + i, n_x)
            got(rx.at[a, from_x], r_rx.at[a, from_x], at(z, from_x))
            add_into(a, y, x * n_z, rx.at[a, from_x])

        each(0, n_x - 1, add)
        each(0, n_z - 1, lambda i: rz_send(a, i).start())

    def reduce_z(a, result):
        total = part[a, y, rows_at(here, rows)].astype(F32)
        for i in range(n_z - 1):
            from_z = lax.rem(z + 1 + i, n_z)
            got(rz.at[a, from_z], r_rz.at[a, from_z], at(from_z, x))
            total = total + rz[a, from_z].astype(F32)
        result[...] = total.astype(BF16)

    exact = lax.Precision.HIGHEST
    each(1, n_z, lambda k: forward(0, k, True))
    open_with(1)
    each(n_z, n_ep, lambda k: forward(0, k, False))
    each(1, n_ep, lambda k: across(0, k))
    each(1, n_z, lambda k: forward(1, k, True))
    gate, upper = project(0, (wg, wu))
    stores = [pltpu.make_async_copy(buf, ref, s_g.at[i]) for i, (buf, ref) in enumerate(((xs, x_out), (cs, c_out)))]
    stores[0].start()
    taken(wa.at[pl.ds(0, count - rows)], r_w)
    weight = dot(member, wa[...], ((1,), (1,)), exact)
    sig = 1.0 / (1.0 + jnp.exp(-gate))
    silu = gate * sig
    hidden = silu * upper
    scaled = weight * hidden
    hand(0, scaled)
    each(n_z, n_ep, lambda k: forward(1, k, False))
    taken(stack.at[pl.ds(0, n_y), pl.ds(0, 3 * high)], r_wt)
    spread(0, 0, 1)
    each(1, n_ep, lambda k: across(1, k))
    (value,) = project(1, (wd,))
    stores[1].start()
    d_hidden = weight * value
    d_gate = d_hidden * upper * (sig * (1.0 + gate * (1.0 - sig)))
    d_up = d_hidden * silu
    hand(1, d_gate)
    hand(2, d_up)
    factors = jnp.concatenate([scaled.astype(BF16), d_gate.astype(BF16), d_up.astype(BF16), label], 1)
    fs[...] = dot(pack, factors, ((1,), (0,))).astype(BF16)
    each(0, n_ep - 1, lambda i: f_send(i).start())
    spread(1, 1, 2)
    reduce_y(0)
    sw[...] = dot((hidden * value).T, member, ((1,), (0,)), exact)
    each(0, n_ep - 1, lambda i: s_send(i).start())
    rw[p] = sw[rows_at(here, rows)]
    reduce_x(0)
    fr[rows_at(p, PACK)] = fs[rows_at(p, PACK)]
    taken(fr.at[pl.ds(0, (n_ep - 1) * PACK)], r_f)
    slot_ids = lax.broadcasted_iota(jnp.int32, (n_ep * PACK, LANES), 1).astype(F32) + 1.0
    chosen = jnp.where(fr[:, 3 * count :].astype(F32) == slot_ids, 1.0, 0.0)
    placing = chosen.T.astype(BF16)[:slots]
    for i in range(3):
        placed[i * slots : (i + 1) * slots] = dot(placing, fr[:, i * count : (i + 1) * count], ((1,), (0,))).astype(BF16)
    for a in range(2):
        fetched = pl.ds(0, quarter + (n_y - 1) * side)
        taken(bufs[a].at[pl.ds(0, (n_z - 1) * rows), fetched], s_z.at[a])
        taken(bufs[a].at[pl.ds(0, n_z * (n_x - 1) * rows), fetched], s_x.at[a])
        taken(bufs[a].at[pl.ds(0, count - rows), pl.ds(0, (n_y - 1) * (quarter - side))], s_y.at[a])
        taken(bufs[a].at[pl.ds(0, count - rows), pl.ds(0, n_y * quarter)], s_c.at[a])
    taken(wa.at[pl.ds(0, count - rows)], s_w)
    taken(fs.at[pl.ds(0, (n_ep - 1) * PACK)], s_f)
    taken(sw.at[pl.ds(0, count - rows)], s_s)
    reduce_y(1)
    taken(rw.at[pl.ds(0, n_ep - 1)], r_s)
    rv[t] = jnp.sum(rw[...], 0)
    each(0, n_tp - 1, lambda i: v_send(i).start())
    reduce_x(1)
    reduce_z(0, out)

    taken(rv.at[pl.ds(0, n_tp - 1)], r_v)
    per_expert = jnp.sum(rv[...], 0)
    choice = lax.broadcasted_iota(jnp.int32, (rows, top), 1)
    picked = jnp.zeros((rows, top), F32)
    for k in range(top):
        value_k = jnp.sum(jnp.where(chosen_by[:, k : k + 1] == experts, per_expert, 0.0), 1, keepdims=True)
        picked = picked + jnp.where(choice == k, value_k, 0.0)
    dwt[...] = picked.T
    reduce_z(1, dtok)
    for store in stores:
        store.wait()
    taken(rv.at[pl.ds(0, n_tp - 1)], s_v)
    for a in range(2):
        taken(part.at[a, pl.ds(0, n_y - 1)], s_ry.at[a])
        taken(part.at[a, 0, pl.ds(0, (n_x - 1) * group)], s_rx.at[a])
        taken(part.at[a, 0, pl.ds(0, (n_z - 1) * rows)], s_rz.at[a])
    for w in range(3):
        taken(crossing.at[pl.ds(0, high)], s_fx.at[w])
    taken(shared, s_wt)


def gradients(out, dtok, dwt, placed, x, c, out_to, dtok_to, dwt_to, grad_gate, grad_up, grad_down):
    @pl.when(pl.program_id(0) == 0)
    def hand_on():
        out_to[...] = out[...]
        dtok_to[...] = dtok[...]
        dwt_to[...] = dwt[...]

    slots = grad_down.shape[0]
    grad_down[...] = dot(placed[:slots], c[...], ((1,), (0,))).astype(BF16)
    both = dot(placed[slots:], x[...], ((1,), (0,))).astype(BF16)
    grad_gate[...] = both[:slots]
    grad_up[...] = both[slots:]


def body(tokens, cotangent, w_gate, w_up, w_down, neuron_expert, neuron_slot, choice_expert, choice_weight):
    n_ep, n_tp = lax.axis_size("ep"), lax.axis_size("tp")
    n_y, n_z, n_x = grid_of(n_tp, n_ep)
    neurons, width = w_gate.shape
    rows = tokens.shape[0]
    count = n_ep * rows
    quarter = width // n_tp
    group = n_z * rows
    high = -(-neurons // PACK) * PACK
    peer_slots = 2 * ((neurons + n_ep - 1) // n_ep)
    capacity = n_ep * peer_slots // E_DEV
    slots = E_DEV * capacity
    assert peer_slots <= PACK and slots <= LANES and E_DEV * n_ep <= LANES

    vmem = pl.BlockSpec(memory_space=pltpu.VMEM)
    anywhere = pl.BlockSpec(memory_space=pl.ANY)
    dma = pltpu.SemaphoreType.DMA
    small = jax.ShapeDtypeStruct((rows, quarter), BF16)
    grad = jax.ShapeDtypeStruct((slots, width), BF16)
    wide = jax.ShapeDtypeStruct((count, width), BF16)
    direct = (small, small, jax.ShapeDtypeStruct(choice_weight.shape[::-1], F32))
    results = pl.pallas_call(
        functools.partial(kernel, n_tp, n_ep),
        out_shape=direct + (jax.ShapeDtypeStruct((3 * slots, count), BF16), wide, wide),
        in_specs=[vmem] * 9,
        out_specs=[vmem] * 4 + [anywhere] * 2,
        scratch_shapes=[
            pltpu.VMEM((count, width), BF16),
            pltpu.VMEM((count, width), BF16),
            pltpu.VMEM((count, LANES), F32),
            pltpu.VMEM((n_ep * PACK, 3 * count + LANES), BF16),
            pltpu.VMEM((n_ep * PACK, 3 * count + LANES), BF16),
            pltpu.VMEM((count, LANES), F32),
            pltpu.VMEM((n_ep, rows, LANES), F32),
            pltpu.VMEM((n_tp, rows, LANES), F32),
            pltpu.VMEM((2, n_y, count, quarter), BF16),
            pltpu.VMEM((n_y, 3 * high, quarter), BF16),
            pltpu.VMEM((n_y, 3 * CORES * high, quarter), BF16),
            pltpu.VMEM((3 * CORES * high, count), F32),
            pltpu.VMEM((2, n_y - 1, n_x, group, quarter), BF16),
            pltpu.VMEM((2, n_x, group, quarter), BF16),
            pltpu.VMEM((2, n_z, rows, quarter), BF16),
            dma((2,)),
            dma((2,)),
            dma((2,)),
            dma((2,)),
            dma((2, n_ep, n_tp)),
            dma((2, n_ep, n_tp)),
            dma((2,)),
        ]
        + [dma] * 8
        + [
            dma,
            dma,
            dma((3,)),
            dma((3,)),
            dma((2,)),
            dma((2, n_y, n_x)),
            dma((2,)),
            dma((2, n_x)),
            dma((2,)),
            dma((2, n_z)),
            dma((2,)),
        ],
        compiler_params=pltpu.CompilerParams(
            collective_id=0, has_side_effects=True, vmem_limit_bytes=62 * 1024 * 1024
        ),
    )(
        tokens, cotangent, w_gate, w_up, w_down,
        neuron_expert.reshape(1, -1), neuron_slot.reshape(1, -1), choice_expert.T, choice_weight.T,
    )
    chunk = min(width, 16 * LANES)

    def whole(ref):
        return pl.BlockSpec(ref.shape, lambda j: (0, 0))

    def columns(height):
        return pl.BlockSpec((height, chunk), lambda j: (0, j))

    output, d_tokens, d_weight, d_gate, d_up, d_down = pl.pallas_call(
        gradients,
        grid=(width // chunk,),
        out_shape=direct + (grad, grad, grad),
        in_specs=[whole(ref) for ref in results[:4]] + [columns(count)] * 2,
        out_specs=[whole(ref) for ref in direct] + [columns(slots)] * 3,
        compiler_params=pltpu.CompilerParams(vmem_limit_bytes=62 * 1024 * 1024),
    )(*results)
    d_weight = d_weight.T

    def expert_blocks(rows_):
        return rows_.reshape(E_DEV, capacity, width)

    return output, d_tokens, d_weight, expert_blocks(d_gate), expert_blocks(d_up), expert_blocks(d_down)


def solution(mesh):
    in_specs = (
        P("ep", None),
        P("ep", None),
        P(("tp", "ep"), None),
        P(("tp", "ep"), None),
        P(("tp", "ep"), None),
        P(("tp", "ep")),
        P(("tp", "ep")),
        P("ep", None),
        P("ep", None),
    )
    out_specs = (
        P("ep", "tp"),
        P("ep", "tp"),
        P("ep", None),
        P("ep", "tp", None),
        P("ep", "tp", None),
        P("ep", "tp", None),
    )
    return jax.shard_map(body, mesh=mesh, in_specs=in_specs, out_specs=out_specs, check_vma=False)
```
